256 devices in a mesh: grp: 8 (over y, core), ctr: 32 (over z, x).
Axes of the slice: x: 4, y: 4, z: 8, core: 2. Of those that a mesh axis runs over, the one named last changes fastest.
Arguments:
- centers: bfloat16 [262144, 1024], P(('grp', 'ctr'))
- coefs: float32 [262144, 1000], P(('grp', 'ctr')), may hold values from -4 to 4
- eigvecs: float32 [65536, 256], P(('grp', 'ctr')), as said below
- eig_weights: float32 [256], replicated, may hold values from 20 to 400
- landmark_index: int32 [65536], P(('grp', 'ctr')), may hold values from 0 to 262143, as said below
- batch_index: int32 [4, 128], replicated, may hold values from 0 to 262143
- targets: float32 [4, 128, 1000], replicated, may hold values from -6 to 6
Outputs:
- new_coefs: float32 [262144, 1000], P(('grp', 'ctr'))
- residuals: float32 [4, 128, 1000], replicated
The draws below stay inside these ranges and needn't reach their ends.
Inputs may be any that keep to these rules, and one draw needn't show every extreme that they name: `landmark_index`: for every block b of 256 consecutive entries, the entries are distinct centers among b * 1024 to b * 1024 + 1023. `eigvecs`: every column sums to zero over all 65536 landmarks, up to rounding: the eigenvectors are orthogonal to the constant vector.
All inputs are finite; a program needn't handle non-finite values.
Results may differ from the reference program's by a relative error of at most 0.0003.
Values sent between devices are 32-bit elements; how exact they have to be, the bound alone decides.
A program may use at most 128 MiB of HBM per device.

```python
import math
import jax
import jax.numpy as jnp
from jax import lax

D = 1024
OUTPUTS = 1000
EIGS = 256
BATCH = 128
STEPS = 4
C_DEV = 1024
S_DEV = 256
CENTERS = 262144
LANDMARKS = 65536


def draw_landmark_index(key, part):
    key = jax.random.fold_in(key, 5)
    blocks = LANDMARKS // S_DEV
    block_keys = jax.random.split(key, blocks)

    def one_block(block_key):
        middle = jax.random.permutation(block_key, C_DEV - 2)[:S_DEV - 2] + 1
        return jnp.concatenate([jnp.zeros((1,), jnp.int32), middle.astype(jnp.int32), jnp.full((1,), C_DEV - 1, jnp.int32)])
    local_rows = jax.vmap(one_block)(block_keys)
    offsets = (jnp.arange(blocks, dtype=jnp.int32) * C_DEV)[:, None]
    return (local_rows + offsets).reshape(-1)


def draw_centers(key, part):
    key = jax.random.fold_in(key, 11)
    values = jax.random.normal(key, (CENTERS, D), jnp.float32) * (1.0 / D) ** 0.5
    return values.astype(jnp.bfloat16)


def draw_eigvecs(key, part):
    key = jax.random.fold_in(key, 12)
    base = jax.random.normal(key, (LANDMARKS, EIGS), jnp.float32)
    following = jnp.roll(base, -1, axis=0)
    return (base - following) * (1.0 / (2.0 * LANDMARKS)) ** 0.5


def plant(array, key, least, top_value):
    place = [jax.random.randint(jax.random.fold_in(key, axis), (), 0, length) for axis, length in enumerate(array.shape)]
    longest = array.shape.index(max(array.shape))
    neighbour = place[:longest] + [(place[longest] + 1) % array.shape[longest]] + place[longest + 1:]
    return array.at[tuple(place)].set(least).at[tuple(neighbour)].set(top_value)


def shard_levels(stream_key, shape, cuts, low, top_value):
    def one(dim, blocks):
        heights = jax.random.uniform(jax.random.fold_in(jax.random.fold_in(stream_key, 6), dim), (blocks,), jnp.float32, low / len(cuts), top_value / len(cuts))
        return jnp.repeat(jnp.exp(heights), shape[dim] // blocks).reshape((-1,) + (1,) * (len(shape) - dim - 1))

    gain = one(*cuts[0])
    for cut in cuts[1:]:
        gain = gain * one(*cut)
    return gain


def gaussian(rng, dims, scale, limit, cuts=(), held_as=jnp.bfloat16):
    result = jax.random.normal(rng, dims, jnp.float32) * scale
    if len(cuts) > 0:
        result = shard_levels(rng, dims, cuts, -0.22, 0.18) * result
    return jnp.clip(result, min=-limit, max=limit).astype(held_as)


def setup_inputs(seed: int = 0) -> dict:
    seeds = jax.random.split(jax.random.key(seed), 8)
    return {
        "centers": draw_centers(jax.random.fold_in(seeds[7], 71), 0),
        "coefs": gaussian(seeds[1], (CENTERS, OUTPUTS), 0.5, 4.0, ((0, 256),), jnp.float32),
        "eigvecs": draw_eigvecs(jax.random.fold_in(seeds[7], 71), 0),
        "eig_weights": jnp.clip(jnp.exp(jax.random.uniform(seeds[3], (EIGS,), jnp.float32, math.log(20.0), math.log(400.0))), 20.0, 400.0),
        "landmark_index": draw_landmark_index(jax.random.fold_in(seeds[7], 71), 0),
        "batch_index": plant(jax.random.randint(seeds[5], (STEPS, BATCH), 0, CENTERS), jax.random.fold_in(seeds[5], 1), 0, CENTERS - 1).astype(jnp.int32),
        "targets": gaussian(seeds[6], (STEPS, BATCH, OUTPUTS), 1.0, 6.0, (), jnp.float32),
    }


floor_sq = 0.01
length_scale = 0.25
step_size = 0.5

def square_norms(rows):
    values = rows.astype(jnp.float32)
    return lax.optimization_barrier(jnp.sum(values * values, axis=1))

def laplace(left_rows, left_sq, right_rows, right_sq):
    inner = jnp.dot(left_rows, right_rows.T, preferred_element_type=jnp.float32)
    squared = left_sq[:, None] + right_sq[None, :] - 2.0 * inner
    return jnp.exp(-jnp.sqrt(jnp.maximum(squared, floor_sq)) / length_scale)

def reference(centers, coefs, eigvecs, eig_weights, landmark_index, batch_index, targets):
    high = lax.Precision.HIGHEST
    center_sq = square_norms(centers)
    landmark_rows = centers[landmark_index]
    landmark_sq = center_sq[landmark_index]
    coeffs = coefs
    collected = []
    for iteration in range(STEPS):
        chosen = batch_index[iteration]
        batch_rows = centers[chosen]
        batch_sq = center_sq[chosen]
        kernel = laplace(batch_rows, batch_sq, centers, center_sq)
        predicted = jnp.dot(kernel, coeffs, precision=high, preferred_element_type=jnp.float32)
        residual = predicted - targets[iteration]
        land_kernel = laplace(landmark_rows, landmark_sq, batch_rows, batch_sq)
        spread = jnp.dot(land_kernel, residual, precision=high, preferred_element_type=jnp.float32)
        projected = jnp.dot(eigvecs.T, spread, precision=high, preferred_element_type=jnp.float32)
        correction = jnp.dot(eigvecs, eig_weights[:, None] * projected, precision=high, preferred_element_type=jnp.float32)
        coeffs = coeffs.at[chosen].add(-step_size * residual).at[landmark_index].add(step_size * correction)
        collected.append(residual)
    return (coeffs, jnp.stack(collected))
```

```python
import functools

import jax
import jax.numpy as jnp
from jax import lax
from jax.experimental import pallas as pl
from jax.experimental.pallas import tpu as pltpu
from jax.sharding import PartitionSpec as P

STEPS = 4
BATCH = 128
EIGS = 256
LANES = 128
SIZES = {"x": 4, "y": 4, "z": 8}

floor_sq = 0.01
length_scale = 0.25
step_size = 0.5

MESH = pl.DeviceIdType.MESH


def allreduce_kernel(sizes, owners, orders, shapes, a_ref, o_ref, *scratch):
    parts = len(owners)
    send, recv = scratch[-2:]
    bufs = scratch[:-2]
    grp, ctr = lax.axis_index("grp"), lax.axis_index("ctr")
    core, y = lax.rem(grp, 2), lax.div(grp, 2)
    z, x = lax.div(ctr, sizes["x"]), lax.rem(ctr, sizes["x"])
    me = {"x": x, "y": y, "z": z}

    def shifted(axis, by):
        return lax.rem(me[axis] + by, sizes[axis])

    def device(axis, by):
        if axis == "c":
            return (y * 2 + 1 - core, ctr)
        to = shifted(axis, by)
        if axis == "x":
            return (grp, z * sizes["x"] + to)
        if axis == "y":
            return (to * 2 + core, ctr)
        return (grp, to * sizes["x"] + x)

    peers = [("c", 1)] + [(axis, by) for axis in "xyz" for by in range(1, sizes[axis])]
    barrier = pltpu.get_barrier_semaphore()
    for axis, by in peers:
        pl.semaphore_signal(barrier, inc=1, device_id=device(axis, by), device_id_type=MESH)
    pl.semaphore_wait(barrier, len(peers))

    count = [0] * parts

    def remote(part, src, dst, to):
        index = count[part]
        count[part] += 1
        return pltpu.make_async_remote_copy(
            src_ref=src,
            dst_ref=dst,
            send_sem=send.at[part, index],
            recv_sem=recv.at[part, index],
            device_id=to,
            device_id_type=MESH,
        )

    def along(ref, dims, axis, index):
        if axis == "z":
            columns = pl.ds(pl.multiple_of(index * LANES, LANES), LANES)
            return ref.at[(slice(None),) * (len(dims) + 1) + (columns,)]
        return ref.at[tuple(index if dim == axis else slice(None) for dim in dims)]

    def region(part, fixed):
        columns = slice(None)
        if "z" in fixed:
            columns = pl.ds(pl.multiple_of(z * LANES, LANES), LANES)
        return o_ref.at[
            part, x if "x" in fixed else slice(None), y if "y" in fixed else slice(None), :, columns
        ]

    every = []

    def mine(part):
        return core == owners[part]

    state = []
    for part in range(parts):
        taken = bufs[8 * part]
        copy = remote(part, a_ref.at[part], taken, device("c", 1))
        pl.when(jnp.logical_not(mine(part)))(copy.start)
        state.append(([copy], a_ref.at[part], [taken], "xy"))

    for phase in range(4):
        nexts = []
        for part in range(parts):
            copies, own, arrived, dims = state[part]
            total = bufs[8 * part + 2 * phase + 1] if phase < 3 else region(part, "xyz")
            sends = []
            if phase < 3:
                axis = orders[part][phase]
                landing = bufs[8 * part + 2 * phase + 2]
                for by in range(1, sizes[axis]):
                    sends.append(
                        remote(
                            part,
                            along(total, dims, axis, shifted(axis, by)),
                            landing.at[by - 1],
                            device(axis, by),
                        )
                    )
                after = dims.replace(axis, "")
                nexts.append(
                    (
                        sends,
                        along(total, dims, axis, me[axis]),
                        [landing.at[by - 1] for by in range(1, sizes[axis])],
                        after,
                    )
                )
            else:
                axis = orders[part][2]
                for by in range(1, sizes[axis]):
                    here = region(part, "xyz")
                    sends.append(remote(part, here, here, device(axis, by)))
                nexts.append((sends, None, None, None))

            @pl.when(mine(part))
            def _(copies=copies, own=own, arrived=arrived, total=total, sends=sends):
                for copy in copies:
                    copy.wait_recv()
                value = own[...]
                for ref in arrived:
                    value = value + ref[...]
                total[...] = value
                for copy in sends:
                    copy.start()

            every.append((part, phase == 0, copies))
        state = nexts

    for phase in range(3):
        nexts = []
        for part in range(parts):
            copies = state[part][0]
            order = orders[part]
            here = region(part, order[: 2 - phase])
            sends = []
            if phase < 2:
                axis = order[1 - phase]
                for by in range(1, sizes[axis]):
                    sends.append(remote(part, here, here, device(axis, by)))
            else:
                sends.append(remote(part, here, here, device("c", 1)))
            nexts.append((sends, None, None, None))

            @pl.when(mine(part))
            def _(copies=copies, sends=sends):
                for copy in copies:
                    copy.wait_recv()
                for copy in sends:
                    copy.start()

            every.append((part, False, copies))
        state = nexts
    for part in range(parts):
        pl.when(jnp.logical_not(mine(part)))(state[part][0][0].wait_recv)
        every.append((part, False, state[part][0]))

    for part, others, copies in every:
        condition = jnp.logical_not(mine(part)) if others else mine(part)

        @pl.when(condition)
        def _(copies=copies):
            for copy in copies:
                copy.wait_send()


def allreduce(a, owners, orders, sizes, collective_id):
    scratch = []
    copies = 2 + 2 * sum(size - 1 for size in sizes.values())
    for order in orders:
        block = list(a.shape[1:])
        dims = "xy"
        scratch += [pltpu.VMEM(tuple(block), a.dtype)] * 2
        for phase, axis in enumerate(order):
            if axis == "z":
                block[-1] = LANES
            else:
                block.pop(dims.index(axis))
                dims = dims.replace(axis, "")
            scratch.append(pltpu.VMEM((sizes[axis] - 1,) + tuple(block), a.dtype))
            if phase < 2:
                scratch.append(pltpu.VMEM(tuple(block), a.dtype))
        scratch.append(pltpu.VMEM((8, LANES), a.dtype))
    scratch += [pltpu.SemaphoreType.DMA((len(owners), copies))] * 2
    return pl.pallas_call(
        functools.partial(allreduce_kernel, sizes, owners, orders, None),
        out_shape=jax.ShapeDtypeStruct(a.shape, a.dtype),
        in_specs=[pl.BlockSpec(memory_space=pltpu.VMEM)],
        out_specs=pl.BlockSpec(memory_space=pltpu.VMEM),
        scratch_shapes=scratch,
        compiler_params=pltpu.CompilerParams(
            collective_id=collective_id, has_side_effects=True, vmem_limit_bytes=40 * 2**20
        ),
    )(a)


def laplace(left_rows, left_sq, right_rows, right_sq):
    inner = lax.dot_general(
        left_rows, right_rows, (((1,), (1,)), ((), ())), preferred_element_type=jnp.float32
    )
    squared = left_sq[:, None] + right_sq[None, :] - 2.0 * inner
    return jnp.exp(-jnp.sqrt(jnp.maximum(squared, floor_sq)) / length_scale)


def fdot(left, right, dims=((1,), (0,)), precision=lax.Precision.HIGH):
    return lax.dot_general(
        left, right, (dims, ((), ())), precision=precision, preferred_element_type=jnp.float32
    )


def body(sizes, centers, coefs, eigvecs, eig_weights, landmark_index, batch_index, targets):
    count, width = centers.shape
    outputs = coefs.shape[1]
    tall = sizes["x"] * sizes["y"] * 8
    total = STEPS * BATCH
    offset = lax.axis_index(("grp", "ctr")) * count
    places = lax.broadcasted_iota(jnp.int32, (1, count), 1)

    owned = (batch_index.reshape(total, 1) - offset) == places
    picked = jnp.dot(
        owned.astype(jnp.bfloat16), centers, preferred_element_type=jnp.float32
    )
    parts = total // tall
    shape = (parts, sizes["x"], sizes["y"], 8, width)
    owners = tuple(p // (parts // 2) for p in range(parts))
    orders = tuple(("xyz", "yxz")[p % 2] for p in range(parts))
    arrived = allreduce(picked.reshape(shape), owners, orders, sizes, 0).reshape(total, width)

    batch_sq = jnp.sum(arrived * arrived, axis=1)
    batch = arrived.astype(jnp.bfloat16)
    values = centers.astype(jnp.float32)
    center_sq = jnp.sum(values * values, axis=1)
    kernel = laplace(batch, batch_sq, centers, center_sq)
    between = laplace(batch, batch_sq, batch, batch_sq)

    at_landmark = (landmark_index.reshape(-1, 1) - offset) == places
    spread = fdot(at_landmark.astype(jnp.float32), eigvecs, ((0,), (0,)), lax.Precision.HIGHEST)

    predicted = jnp.pad(fdot(kernel, coefs), ((0, 0), (0, width - outputs)))
    gradient = fdot(kernel, spread)
    across = width // EIGS
    gradient = gradient.reshape(across, total // across, EIGS).transpose(1, 0, 2)
    extra = gradient.reshape(total // across, width)
    packed = jnp.concatenate([predicted, extra], axis=0)
    parts = packed.shape[0] // tall
    shape = (parts, sizes["x"], sizes["y"], 8, width)
    more = extra.shape[0] // tall
    owners = owners + (0,) * more
    orders = orders + ("zxy",) * more
    summed = allreduce(packed.reshape(shape), owners, orders, sizes, 1).reshape(packed.shape)

    predicted = summed[:total, :outputs]
    gradient = summed[total:].reshape(total // across, across, EIGS).transpose(1, 0, 2)
    gradient = gradient.reshape(total, EIGS)
    weighted = gradient * (step_size * eig_weights)[None, :]
    effect = fdot(weighted, gradient, ((1,), (1,))) - step_size * between
    residuals = []
    for step in range(STEPS):
        rows = slice(step * BATCH, (step + 1) * BATCH)
        residual = predicted[rows] - targets[step]
        if step > 0:
            residual = residual + fdot(
                effect[rows, : step * BATCH],
                jnp.concatenate(residuals, axis=0),
                precision=lax.Precision.HIGHEST,
            )
        residuals.append(residual)
    residual = jnp.concatenate(residuals, axis=0)
    update = fdot(spread, weighted, ((1,), (1,))) - step_size * owned.T.astype(jnp.float32)
    return coefs + fdot(update, residual), residual.reshape(STEPS, BATCH, outputs)


def solution(mesh, sizes=SIZES):
    in_specs = (
        P(("grp", "ctr"), None),
        P(("grp", "ctr"), None),
        P(("grp", "ctr"), None),
        P(),
        P(("grp", "ctr")),
        P(),
        P(),
    )
    out_specs = (P(("grp", "ctr"), None), P())
    return jax.shard_map(
        functools.partial(body, sizes),
        mesh=mesh,
        in_specs=in_specs,
        out_specs=out_specs,
        check_vma=False,
    )
```

```python
import functools

import jax
import jax.numpy as jnp
from jax import lax
from jax.experimental import pallas as pl
from jax.experimental.pallas import tpu as pltpu
from jax.sharding import PartitionSpec as P

STEPS = 4
LANES = 128
TILE = 256
MIB = 2**20
SIZES = {"x": 4, "y": 4, "z": 8}

floor_sq = 0.01
length_scale = 0.25
step_size = 0.5

MESH = pl.DeviceIdType.MESH
f32, bf16 = jnp.float32, jnp.bfloat16
NT = (((1,), (1,)), ((), ()))
NN = (((1,), (0,)), ((), ()))


def dot(left, right, dims=NN):
    return lax.dot_general(left, right, dims, preferred_element_type=f32)


def split(value):
    high = value.astype(bf16)
    return high, (value - high.astype(f32)).astype(bf16)


def dot3(left, right, dims=NN):
    return dot(left[0], right[0], dims) + (dot(left[0], right[1], dims) + dot(left[1], right[0], dims))


class Sum:
    def __init__(self, place, theirs, own, out, order, bufs, send, recv):
        sizes, me, device = place
        count = [0]

        def remote(src, dst, to):
            index = count[0]
            count[0] += 1
            return pltpu.make_async_remote_copy(
                src_ref=src,
                dst_ref=dst,
                send_sem=send.at[index],
                recv_sem=recv.at[index],
                device_id=to,
                device_id_type=MESH,
            )

        def columns(index):
            return pl.ds(pl.multiple_of(index * LANES, LANES), LANES)

        def along(ref, dims, axis, index):
            if axis == "z":
                return ref.at[(slice(None),) * (len(dims) + 1) + (columns(index),)]
            return ref.at[tuple(index if dim == axis else slice(None) for dim in dims)]

        def region(fixed):
            return out.at[
                me["x"] if "x" in fixed else slice(None),
                me["y"] if "y" in fixed else slice(None),
                slice(None),
                columns(me["z"]) if "z" in fixed else slice(None),
            ]

        def to(axis, by):
            return lax.rem(me[axis] + by, sizes[axis])

        self.core = remote(theirs, bufs[0], device("c", 1))
        self.stages = []
        copies, terms, dims = [self.core], [own, bufs[0]], "xy"
        for phase in range(3):
            axis = order[phase]
            total, landing = bufs[1 + 2 * phase], bufs[2 + 2 * phase]
            hops = range(1, sizes[axis])
            sends = [
                remote(along(total, dims, axis, to(axis, by)), landing.at[by - 1], device(axis, by))
                for by in hops
            ]
            self.stages.append((copies, terms, total, sends))
            terms = [along(total, dims, axis, me[axis])] + [landing.at[by - 1] for by in hops]
            copies, dims = sends, dims.replace(axis, "")
        total = region("xyz")
        for phase in range(3):
            axis = order[2 - phase]
            here = region(order[: 3 - phase])
            sends = [remote(here, here, device(axis, by)) for by in range(1, sizes[axis])]
            self.stages.append((copies, terms, total, sends))
            copies, terms, total = sends, None, None
        self.back = remote(out, out, device("c", 1))
        self.stages.append((copies, None, None, [self.back]))

    def run(self, stage):
        copies, terms, total, sends = self.stages[stage]
        for copy in copies:
            copy.wait_recv()
        if terms is not None:
            value = terms[0][...]
            for term in terms[1:]:
                value = value + term[...]
            total[...] = value
        for copy in sends:
            copy.start()

    def finish(self):
        for stage in self.stages:
            for copy in stage[3]:
                copy.wait_send()


def sum_scratch(sizes, order, block):
    block = list(block)
    dims = "xy"
    scratch = [pltpu.VMEM(tuple(block), f32)] * 2
    for phase, axis in enumerate(order):
        if axis == "z":
            block[-1] = LANES
        else:
            block.pop(dims.index(axis))
            dims = dims.replace(axis, "")
        scratch.append(pltpu.VMEM((sizes[axis] - 1,) + tuple(block), f32))
        if phase < 2:
            scratch.append(pltpu.VMEM(tuple(block), f32))
    return scratch


ORDERS_X = ("xyz", "yxz")
ORDERS_P = ("xyz", "yxz", "zxy")
BUFS = 7


def main_kernel(
    sizes,
    centers,
    coefs_hbm,
    eigvecs,
    weights,
    landmarks,
    batch_index,
    targets_hbm,
    residual,
    update_high,
    update_low,
    coefs,
    targets,
    right_high,
    right_low,
    center_sq,
    picked,
    arrived,
    points,
    batch,
    kernel,
    batch_sq,
    between,
    predicted,
    gradient,
    predicted_sum,
    gradient_sum,
    effect_high,
    effect_low,
    residual_high,
    residual_low,
    local_sem,
    send_x,
    recv_x,
    send_p,
    recv_p,
    *bufs,
):
    grp, ctr = lax.axis_index("grp"), lax.axis_index("ctr")
    core, y = lax.rem(grp, 2), lax.div(grp, 2)
    z, x = lax.div(ctr, sizes["x"]), lax.rem(ctr, sizes["x"])
    me = {"x": x, "y": y, "z": z}

    def device(axis, by):
        if axis == "c":
            return (y * 2 + 1 - core, ctr)
        to = lax.rem(me[axis] + by, sizes[axis])
        if axis == "x":
            return (grp, z * sizes["x"] + to)
        if axis == "y":
            return (to * 2 + core, ctr)
        return (grp, to * sizes["x"] + x)

    place = (sizes, me, device)
    peers = [("c", 1)] + [(axis, by) for axis in "xyz" for by in range(1, sizes[axis])]
    barrier = pltpu.get_barrier_semaphore()
    for axis, by in peers:
        pl.semaphore_signal(barrier, inc=1, device_id=device(axis, by), device_id_type=MESH)

    count, width = centers.shape
    outputs = coefs_hbm.shape[0]
    eigs = eigvecs.shape[1]
    rows = batch_index.shape[1]
    coefs_in = pltpu.make_async_copy(coefs_hbm, coefs.at[:outputs], local_sem.at[0])
    targets_in = pltpu.make_async_copy(targets_hbm, targets.at[:, :outputs], local_sem.at[1])
    coefs_in.start()
    targets_in.start()
    coefs[outputs:, :] = jnp.zeros((width - outputs, count), f32)
    targets[:, outputs:, :] = jnp.zeros((STEPS, width - outputs, rows), f32)
    pair = 2 * rows
    block = (2,) + tuple(picked.shape[1:])
    row_tile, tile, out_tile = min(TILE, count), min(TILE, width), min(2 * TILE, width)
    offset = (grp * lax.axis_size("ctr") + ctr) * count

    def tiles(length, size):
        def loop(step):
            @pl.loop(0, length // size)
            def _(index):
                step(pl.ds(pl.multiple_of(index * size, size), size))

        return loop

    for step in range(STEPS):
        local = jnp.broadcast_to(batch_index[step : step + 1, :] - offset, (LANES, rows))
        points[step * rows : (step + 1) * rows, :] = local.T

    def is_owned(here, length, start, size):
        local = points[here, 0:1] - start
        return local == lax.broadcasted_iota(jnp.int32, (length, size), 1)

    def pick(index):
        owned = is_owned(pl.ds(pl.multiple_of(index * pair, pair), pair), pair, 0, count)
        owned = jnp.where(owned, 1.0, 0.0).astype(bf16)

        @tiles(width, tile)
        def _(columns):
            value = dot(owned, centers[:, columns])
            picked[pl.ds(index * 2, 2), :, :, :, columns] = value.reshape(block[:-1] + (tile,))

    mine, other = core, 1 - core
    sums_x = [
        Sum(
            place,
            picked.at[other * 2 + k],
            picked.at[mine * 2 + k],
            arrived.at[mine * 2 + k],
            ORDERS_X[k],
            bufs[k * BUFS : (k + 1) * BUFS],
            send_x.at[k],
            recv_x.at[k],
        )
        for k in range(2)
    ]
    pick(other)
    pl.semaphore_wait(barrier, len(peers))
    for part in sums_x:
        part.core.start()
    pick(mine)
    for part in sums_x:
        part.run(0)

    coefs_in.wait()

    @tiles(width, tile // 2)
    def _(here):
        right_high[here, :], right_low[here, :] = split(coefs[here, :])

    for part in sums_x:
        part.run(1)

    eig_high, eig_low = split(eigvecs[...].T)

    @tiles(count, row_tile)
    def _(here):
        local = landmarks[...] - offset - here.start
        at = jnp.where(
            local == lax.broadcasted_iota(jnp.int32, (row_tile, landmarks.shape[1]), 0), 1.0, 0.0
        ).astype(bf16)
        right_high[width:, here] = dot(eig_high, at, NT).astype(bf16)
        right_low[width:, here] = dot(eig_low, at, NT).astype(bf16)

    for part in sums_x:
        part.run(2)
    ones = jnp.ones((8, width), bf16)

    @tiles(count, row_tile)
    def _(here):
        value = centers[here, :].astype(f32)
        high, low = split(value * value)
        center_sq[:, here] = dot(ones, high, NT) + dot(ones, low, NT)

    for stage in range(3, 7):
        for part in sums_x:
            part.run(stage)

    sums_p = [
        Sum(
            place,
            predicted.at[mine * 2 + k],
            predicted.at[other * 2 + k],
            predicted_sum.at[other * 2 + k],
            ORDERS_P[k],
            bufs[(2 + k) * BUFS : (3 + k) * BUFS],
            send_p.at[k],
            recv_p.at[k],
        )
        for k in range(2)
    ]
    sum_g = Sum(
        place, gradient, gradient, gradient_sum, ORDERS_P[2], bufs[4 * BUFS : 5 * BUFS], send_p.at[2], recv_p.at[2]
    )

    def laplace(left_sq, right_sq, inner):
        squared = left_sq + right_sq - 2.0 * inner
        return jnp.exp(jnp.sqrt(jnp.maximum(squared, floor_sq)) * (-1.0 / length_scale))

    def predict(index):
        here = pl.ds(pl.multiple_of(index * pair, pair), pair)
        value = arrived[pl.ds(index * 2, 2)].reshape(pair, width)
        value_sq = jnp.sum(value * value, axis=1, keepdims=True)
        batch_sq[here, :] = jnp.broadcast_to(value_sq, (pair, LANES))
        batch[here, :] = value.astype(bf16)

        @tiles(count, row_tile)
        def _(columns):
            inner = dot(batch[here, :], centers[columns, :], NT)
            high, low = split(laplace(batch_sq[here, 0:1], center_sq[0:1, columns], inner))
            kernel[:pair, columns] = high
            kernel[pair:, columns] = low

        both = dot(kernel[...], right_high[width:, :], NT)
        value = both[:pair] + (both[pair:] + dot(kernel[:pair, :], right_low[width:, :], NT))
        for k in range(2):
            columns = pl.ds(pl.multiple_of((index * 2 + k) * eigs, eigs), eigs)
            gradient[:, :, :, columns] = value[k * rows : (k + 1) * rows].reshape(block[1:-1] + (eigs,))

        @pl.loop(0, width // out_tile)
        def _(step):
            here = pl.ds(pl.multiple_of(step * out_tile, out_tile), out_tile)
            both = dot(right_high[here, :], kernel[...], NT)
            value = both[:, :pair] + (both[:, pair:] + dot(right_low[here, :], kernel[:pair, :], NT))
            for j in range(out_tile // LANES):
                columns = pl.ds(pl.multiple_of(step * out_tile + j * LANES, LANES), LANES)
                for k in range(2):
                    piece = value[j * LANES : (j + 1) * LANES, k * rows : (k + 1) * rows]
                    predicted[index * 2 + k, :, :, :, columns] = piece.reshape(block[1:-1] + (rows,))

    predict(mine)
    for part in sums_p:
        part.core.start()
    for part in sums_x:
        part.back.wait_recv()
    predict(other)
    pl.when(core == 1)(sum_g.core.start)

    def both(stage):
        for part in sums_p:
            part.run(stage)

    def extra(stage):
        pl.when(core == 0)(functools.partial(sum_g.run, stage))

    both(0)
    extra(0)

    total = STEPS * rows
    value = batch[...].astype(f32)
    high, low = split(value * value)
    points_sq = (dot(ones, high, NT) + dot(ones, low, NT))[0:1, :]

    @tiles(total, rows)
    def _(here):
        inner = dot(batch[here, :], batch[...], NT)
        between[here, :] = laplace(batch_sq[here, 0:1], points_sq, inner)

    for stage in range(1, 7):
        both(stage)
        extra(stage)

    pl.when(core == 1)(sum_g.back.wait_recv)
    targets_in.wait()
    projection = gradient_sum[...].reshape(rows, width)
    scale = step_size * weights[...]
    plain, weighted = [], []
    for step in range(STEPS):
        value = projection[:, step * eigs : (step + 1) * eigs]
        plain.append(split(value))
        weighted.append(split(value * scale))
    for step in range(STEPS):
        now = slice(step * rows, (step + 1) * rows)

        @tiles(count, row_tile)
        def _(here, now=now, step=step):
            value = dot3(weighted[step], (right_high[width:, here], right_low[width:, here]))
            value = value - jnp.where(is_owned(now, rows, here.start, row_tile), step_size, 0.0)
            update_high[now, here], update_low[now, here] = split(value)

        for past in range(step):
            then = slice(past * rows, (past + 1) * rows)
            value = dot3(weighted[step], plain[past], NT) - step_size * between[now, then]
            effect_high[now, then], effect_low[now, then] = split(value)
    for part in sums_p:
        part.back.wait_recv()
    for step in range(STEPS):
        now, then = slice(step * rows, (step + 1) * rows), slice(0, step * rows)
        pieces = [
            predicted_sum[step, :, :, :, j * LANES : (j + 1) * LANES].reshape(rows, rows)
            for j in range(width // LANES)
        ]
        value = jnp.concatenate(pieces, axis=0) - targets[step]
        if step > 0:
            value = value + dot3(
                (residual_high[:, then], residual_low[:, then]), (effect_high[now, then], effect_low[now, then]), NT
            )
        residual[step] = value[:outputs]
        if step < STEPS - 1:
            residual_high[:, now], residual_low[:, now] = split(value)

    for part in sums_x + sums_p:
        part.core.wait_send()
        part.finish()
    pl.when(core == 1)(sum_g.core.wait_send)
    pl.when(core == 0)(sum_g.finish)


def update_kernel(update_high, update_low, coefs, residual, new_coefs, residuals):
    residuals[...] = residual[...]
    value = split(jnp.concatenate([residual[step] for step in range(STEPS)], axis=1))
    new_coefs[...] = coefs[...] + dot3(value, (update_high[...], update_low[...]))


def body(sizes, centers, coefs, eigvecs, eig_weights, landmark_index, batch_index, targets):
    count, width = centers.shape
    outputs = coefs.shape[1]
    eigs = eigvecs.shape[1]
    rows = batch_index.shape[1]
    total = STEPS * rows
    block = (sizes["x"], sizes["y"], 8, width)
    copies = 2 + 2 * sum(size - 1 for size in sizes.values())
    bufs = []
    for order in ORDERS_X + ORDERS_P:
        bufs += sum_scratch(sizes, order, block)
    dma = pltpu.SemaphoreType.DMA
    vmem = pl.BlockSpec(memory_space=pltpu.VMEM)
    hbm = pl.BlockSpec(memory_space=pl.ANY)
    residual, update_high, update_low = pl.pallas_call(
        functools.partial(main_kernel, sizes),
        out_shape=[
            jax.ShapeDtypeStruct((STEPS, outputs, rows), f32),
            jax.ShapeDtypeStruct((total, count), bf16),
            jax.ShapeDtypeStruct((total, count), bf16),
        ],
        in_specs=[vmem, hbm, vmem, vmem, vmem, vmem, hbm],
        out_specs=[vmem] * 3,
        scratch_shapes=[
            pltpu.VMEM((width, count), f32),
            pltpu.VMEM((STEPS, width, rows), f32),
            pltpu.VMEM((width + eigs, count), bf16),
            pltpu.VMEM((width + eigs, count), bf16),
            pltpu.VMEM((8, count), f32),
            pltpu.VMEM((STEPS,) + block, f32),
            pltpu.VMEM((STEPS,) + block, f32),
            pltpu.VMEM((total, LANES), jnp.int32),
            pltpu.VMEM((total, width), bf16),
            pltpu.VMEM((4 * rows, count), bf16),
            pltpu.VMEM((total, LANES), f32),
            pltpu.VMEM((total, total), f32),
            pltpu.VMEM((STEPS,) + block, f32),
            pltpu.VMEM(block, f32),
            pltpu.VMEM((STEPS,) + block, f32),
            pltpu.VMEM(block, f32),
            pltpu.VMEM((total, total), bf16),
            pltpu.VMEM((total, total), bf16),
            pltpu.VMEM((width, total), bf16),
            pltpu.VMEM((width, total), bf16),
            dma((2,)),
            dma((2, copies)),
            dma((2, copies)),
            dma((3, copies)),
            dma((3, copies)),
        ]
        + bufs,
        compiler_params=pltpu.CompilerParams(
            collective_id=0, has_side_effects=True, vmem_limit_bytes=56 * MIB
        ),
        name="predict",
    )(
        centers,
        coefs.T,
        eigvecs,
        eig_weights.reshape(1, eigs),
        landmark_index.reshape(1, -1),
        batch_index,
        targets.transpose(0, 2, 1),
    )

    tile = next(tile for tile in (200, 8, outputs) if outputs % tile == 0)
    new_coefs, residuals = pl.pallas_call(
        update_kernel,
        grid=(outputs // tile,),
        out_shape=[
            jax.ShapeDtypeStruct((outputs, count), f32),
            jax.ShapeDtypeStruct((STEPS, outputs, rows), f32),
        ],
        in_specs=[
            pl.BlockSpec((total, count), lambda i: (0, 0)),
            pl.BlockSpec((total, count), lambda i: (0, 0)),
            pl.BlockSpec((tile, count), lambda i: (i, 0)),
            pl.BlockSpec((STEPS, tile, rows), lambda i: (0, i, 0)),
        ],
        out_specs=[
            pl.BlockSpec((tile, count), lambda i: (i, 0)),
            pl.BlockSpec((STEPS, tile, rows), lambda i: (0, i, 0)),
        ],
        compiler_params=pltpu.CompilerParams(vmem_limit_bytes=60 * MIB),
        name="update",
    )(update_high, update_low, coefs.T, residual)
    return new_coefs.T, residuals.transpose(0, 2, 1)


def solution(mesh, sizes=SIZES):
    in_specs = (
        P(("grp", "ctr"), None),
        P(("grp", "ctr"), None),
        P(("grp", "ctr"), None),
        P(),
        P(("grp", "ctr")),
        P(),
        P(),
    )
    out_specs = (P(("grp", "ctr"), None), P())
    return jax.shard_map(
        functools.partial(body, sizes),
        mesh=mesh,
        in_specs=in_specs,
        out_specs=out_specs,
        check_vma=False,
    )
```

```python
import functools

import jax
import jax.numpy as jnp
from jax import lax
from jax.experimental import pallas as pl
from jax.experimental.pallas import tpu as pltpu
from jax.sharding import PartitionSpec as P

STEPS = 4
LANES = 128
TILE = 256
MIB = 2**20
SIZES = {"x": 4, "y": 4, "z": 8}

floor_sq = 0.01
length_scale = 0.25
step_size = 0.5

MESH = pl.DeviceIdType.MESH
f32, bf16 = jnp.float32, jnp.bfloat16
NT = (((1,), (1,)), ((), ()))
NN = (((1,), (0,)), ((), ()))


def dot(left, right, dims=NN):
    return lax.dot_general(left, right, dims, preferred_element_type=f32)


def split(value):
    high = value.astype(bf16)
    return high, (value - high.astype(f32)).astype(bf16)


def dot3(left, right, dims=NN):
    return dot(left[0], right[0], dims) + (dot(left[0], right[1], dims) + dot(left[1], right[0], dims))


def span(index):
    return pl.ds(pl.multiple_of(index * LANES, LANES), LANES)


class Copies:
    def __init__(self, place, sems, index, like):
        self.send, self.recv = (sem.at[index] for sem in sems)
        self.like, self.copies = like, []
        self.device = place[2]

    def to(self, axis, by, src, dst):
        self.copies.append(self.copy(axis, by, src, dst))

    def copy(self, axis, by, src, dst):
        return pltpu.make_async_remote_copy(
            src_ref=src,
            dst_ref=dst,
            send_sem=self.send,
            recv_sem=self.recv,
            device_id=self.device(axis, by),
            device_id_type=MESH,
        )

    def start(self):
        for copy in self.copies:
            copy.start()

    def wait_recv(self):
        if self.copies:
            self.copy("c", 1, self.like, self.like).wait_recv()

    def wait_send(self):
        if self.copies:
            self.copy("c", 1, self.like, self.like).wait_send()


def add(terms, into):
    value = terms[0][...]
    for term in terms[1:]:
        value = value + term[...]
    into[...] = value


class Sum:
    def __init__(self, place, theirs, own, out, order, bufs, sems):
        sizes, me, device = place

        def along(ref, dims, axis, index):
            if axis == "z":
                return ref.at[(slice(None),) * (len(dims) + 1) + (span(index),)]
            return ref.at[tuple(index if dim == axis else slice(None) for dim in dims)]

        def region(fixed):
            return out.at[
                me["x"] if "x" in fixed else slice(None),
                me["y"] if "y" in fixed else slice(None),
                slice(None),
                span(me["z"]) if "z" in fixed else slice(None),
            ]

        self.core = Copies(place, sems, 0, bufs[0])
        self.core.to("c", 1, theirs, bufs[0])
        self.stages = []
        copies, terms, dims = self.core, [own, bufs[0]], "xy"
        for phase in range(3):
            axis = order[phase]
            total, landing = bufs[1 + 2 * phase], bufs[2 + 2 * phase]
            sends = Copies(place, sems, 1 + phase, landing)
            for by in range(1, sizes[axis]):
                index = lax.rem(me[axis] + by, sizes[axis])
                sends.to(axis, by, along(total, dims, axis, index), landing.at[by - 1])
            self.stages.append((copies, terms, total, sends))
            terms = [along(total, dims, axis, me[axis])] + [landing.at[by - 1] for by in range(1, sizes[axis])]
            copies, dims = sends, dims.replace(axis, "")
        total = region("xyz")
        for phase in range(3):
            axis = order[2 - phase]
            here = region(order[: 3 - phase])
            sends = Copies(place, sems, 4 + phase, bufs[6 - 2 * phase])
            for by in range(1, sizes[axis]):
                sends.to(axis, by, here, here)
            self.stages.append((copies, terms, total, sends))
            copies, terms, total = sends, None, None
        self.back = Copies(place, sems, 7, bufs[0])
        self.back.to("c", 1, out, out)
        self.stages.append((copies, None, None, self.back))

    def run(self, stage):
        copies, terms, total, sends = self.stages[stage]
        copies.wait_recv()
        if terms is not None:
            add(terms, total)
        sends.start()

    def finish(self):
        for stage in self.stages:
            stage[3].wait_send()


class Pair:
    def __init__(self, place, theirs, own, out, bufs, sems):
        sizes, me, device = place
        self.taken, self.total0, landing0, self.total1, landing1, self.total2, landing2 = bufs
        self.far = sorted(range(sizes["x"]), key=lambda by: -min(by, sizes["x"] - by))

        def first(ref, k, index):
            return ref.at[k, index] if k == 0 else ref.at[k, :, index]

        def to(axis, by):
            return lax.rem(me[axis] + by, sizes[axis])

        self.core, self.one, self.two, self.up2, self.up1, self.back = [], [], [], [], [], []
        self.terms1, self.terms2, self.sums = [], [], []
        for k in range(2):
            axis, other = ("x", "y") if k == 0 else ("y", "x")
            base, side = 11 * k, sizes[axis]
            core, up1 = {}, {}
            one = Copies(place, sems, base + 1, landing0.at[k])
            two = Copies(place, sems, base + 2, landing1.at[k])
            up2 = Copies(place, sems, base + 3, landing1.at[k])
            back = Copies(place, sems, base, self.taken.at[k])
            for by in range(side):
                core[by] = Copies(place, sems, base + 4 + by, landing0.at[k, 0])
                index = to(axis, by)
                core[by].to("c", 1, first(theirs, k, index), first(self.taken, k, index))
                here = first(out, k, index)
                back.to("c", 1, here, here)
            here = out.at[k, me["x"], me["y"]]
            for by in range(1, sizes[other]):
                two.to(other, by, self.total1.at[k, to(other, by)], landing1.at[k, by - 1])
                up2.to(other, by, here, here)
            here = first(out, k, me[axis])
            for by in range(1, sizes[axis]):
                one.to(axis, by, first(self.total0, k, to(axis, by)), landing0.at[k, by - 1])
                up1[by] = Copies(place, sems, base + 7 + by, landing0.at[k, 0])
                up1[by].to(axis, by, here, here)
            self.sums.append(
                [
                    [first(ref, k, to(axis, by)) for ref in (own, self.taken, self.total0)]
                    for by in range(side)
                ]
            )
            self.terms1.append(
                [first(self.total0, k, me[axis])] + [landing0.at[k, by - 1] for by in range(1, sizes[axis])]
            )
            self.terms2.append(
                [self.total1.at[k, me[other]]] + [landing1.at[k, by - 1] for by in range(1, sizes[other])]
            )
            self.core.append(core)
            self.one.append(one)
            self.two.append(two)
            self.up2.append(up2)
            self.up1.append(up1)
            self.back.append(back)
        self.down = Copies(place, sems, 22, landing2)
        self.up = Copies(place, sems, 23, landing2)
        self.mine = out.at[:, me["x"], me["y"], :, span(me["z"])]
        for by in range(1, sizes["z"]):
            self.down.to("z", by, self.total2.at[:, :, span(to("z", by))], landing2.at[by - 1])
            self.up.to("z", by, self.mine, self.mine)
        self.last = [self.total2.at[:, :, span(me["z"])]] + [landing2.at[by - 1] for by in range(1, sizes["z"])]

    def start_core(self):
        for by in self.far:
            for k in range(2):
                self.core[k][by].start()

    def run(self, stage):
        if stage == 0:
            for by in self.far:
                for k in range(2):
                    self.core[k][by].wait_recv()
                    own, taken, total = self.sums[k][by]
                    add([own, taken], total)
                    if by > 0:
                        self.one[k].copies[by - 1].start()
        if stage == 6:
            for by in reversed(self.far[:-1]):
                for k in range(2):
                    self.up1[k][by].wait_recv()
                    self.back[k].copies[len(self.far) - by].start()
        if stage == 3:
            self.down.wait_recv()
            add(self.last, self.mine)
            self.up.start()
        elif stage == 4:
            self.up.wait_recv()
        for k in range(2):
            if stage == 1:
                self.one[k].wait_recv()
                add(self.terms1[k], self.total1.at[k])
                self.two[k].start()
            elif stage == 2:
                self.two[k].wait_recv()
                add(self.terms2[k], self.total2.at[k])
            elif stage == 4:
                self.up2[k].start()
            elif stage == 5:
                self.up2[k].wait_recv()
                for by in self.far[:-1]:
                    self.up1[k][by].start()
                self.back[k].copies[0].start()
        if stage == 2:
            self.down.start()

    def finish(self):
        for core in self.core:
            for copies in core.values():
                copies.wait_send()
        for copies in self.one + self.two + [self.down, self.up] + self.up2:
            copies.wait_send()

    def finish_last(self):
        for up1 in self.up1:
            for copies in up1.values():
                copies.wait_send()
        for copies in self.back:
            copies.wait_send()


def sum_scratch(sizes, order, block):
    block = list(block)
    dims = "xy"
    scratch = [pltpu.VMEM(tuple(block), f32)] * 2
    for phase, axis in enumerate(order):
        if axis == "z":
            block[-1] = LANES
        else:
            block.pop(dims.index(axis))
            dims = dims.replace(axis, "")
        scratch.append(pltpu.VMEM((sizes[axis] - 1,) + tuple(block), f32))
        if phase < 2:
            scratch.append(pltpu.VMEM(tuple(block), f32))
    return scratch


def pair_scratch(sizes, block):
    side, deep, rows, width = block
    shapes = [
        (2,) + block,
        (2,) + block,
        (2, side - 1, side, rows, width),
        (2, side, rows, width),
        (2, side - 1, rows, width),
        (2, rows, width),
        (sizes["z"] - 1, 2, rows, LANES),
    ]
    return [pltpu.VMEM(shape, f32) for shape in shapes]


EXTRA = "zxy"
BUFS = 7


def main_kernel(
    sizes,
    centers,
    coefs_hbm,
    eigvecs,
    weights,
    landmarks,
    batch_index,
    targets_hbm,
    residual,
    update_high,
    update_low,
    coefs,
    targets,
    right_high,
    right_low,
    center_sq,
    picked,
    arrived,
    points,
    batch,
    kernel,
    batch_sq,
    between,
    predicted,
    gradient,
    predicted_sum,
    gradient_sum,
    effect_high,
    effect_low,
    residual_high,
    residual_low,
    local_sem,
    send_x,
    recv_x,
    send_p,
    recv_p,
    send_g,
    recv_g,
    *bufs,
):
    grp, ctr = lax.axis_index("grp"), lax.axis_index("ctr")
    core, y = lax.rem(grp, 2), lax.div(grp, 2)
    z, x = lax.div(ctr, sizes["x"]), lax.rem(ctr, sizes["x"])
    me = {"x": x, "y": y, "z": z}

    def device(axis, by):
        if axis == "c":
            return (y * 2 + 1 - core, ctr)
        to = lax.rem(me[axis] + by, sizes[axis])
        if axis == "x":
            return (grp, z * sizes["x"] + to)
        if axis == "y":
            return (to * 2 + core, ctr)
        return (grp, to * sizes["x"] + x)

    place = (sizes, me, device)
    peers = [("c", 1)] + [(axis, by) for axis in "xyz" for by in range(1, sizes[axis])]
    barrier = pltpu.get_barrier_semaphore()
    for axis, by in peers:
        pl.semaphore_signal(barrier, inc=1, device_id=device(axis, by), device_id_type=MESH)

    count, width = centers.shape
    outputs = coefs_hbm.shape[0]
    eigs = eigvecs.shape[1]
    rows = batch_index.shape[1]
    coefs_in = pltpu.make_async_copy(coefs_hbm, coefs.at[:outputs], local_sem.at[0])
    targets_in = pltpu.make_async_copy(targets_hbm, targets.at[:, :outputs], local_sem.at[1])
    coefs_in.start()
    targets_in.start()
    coefs[outputs:, :] = jnp.zeros((width - outputs, count), f32)
    targets[:, outputs:, :] = jnp.zeros((STEPS, width - outputs, rows), f32)
    pair = 2 * rows
    block = (2,) + tuple(picked.shape[1:])
    row_tile, tile, out_tile = min(TILE, count), min(TILE, width), max(width // 2, LANES)
    offset = (grp * lax.axis_size("ctr") + ctr) * count

    def tiles(length, size):
        def loop(step):
            @pl.loop(0, length // size)
            def _(index):
                step(pl.ds(pl.multiple_of(index * size, size), size))

        return loop

    for step in range(STEPS):
        local = jnp.broadcast_to(batch_index[step : step + 1, :] - offset, (LANES, rows))
        points[step * rows : (step + 1) * rows, :] = local.T

    def is_owned(here, length, start, size):
        local = points[here, 0:1] - start
        return local == lax.broadcasted_iota(jnp.int32, (length, size), 1)

    def pick(index):
        owned = is_owned(pl.ds(pl.multiple_of(index * pair, pair), pair), pair, 0, count)
        owned = jnp.where(owned, 1.0, 0.0).astype(bf16)

        @tiles(width, tile)
        def _(columns):
            value = dot(owned, centers[:, columns])
            picked[pl.ds(index * 2, 2), :, :, :, columns] = value.reshape(block[:-1] + (tile,))

    mine, other = core, 1 - core
    def two(ref, index):
        return ref.at[pl.ds(index * 2, 2)]

    sum_x = Pair(place, two(picked, other), two(picked, mine), two(arrived, mine), bufs[:BUFS], (send_x, recv_x))
    pick(other)
    pl.semaphore_wait(barrier, len(peers))
    sum_x.start_core()
    pick(mine)
    sum_x.run(0)

    coefs_in.wait()

    @tiles(width, tile // 2)
    def _(here):
        right_high[here, :], right_low[here, :] = split(coefs[here, :])

    sum_x.run(1)

    eig_high, eig_low = split(eigvecs[...].T)

    @tiles(count, row_tile)
    def _(here):
        local = landmarks[...] - offset - here.start
        at = jnp.where(
            local == lax.broadcasted_iota(jnp.int32, (row_tile, landmarks.shape[1]), 0), 1.0, 0.0
        ).astype(bf16)
        right_high[width:, here] = dot(eig_high, at, NT).astype(bf16)
        right_low[width:, here] = dot(eig_low, at, NT).astype(bf16)

    sum_x.run(2)
    ones = jnp.ones((8, width), bf16)

    @tiles(count, row_tile)
    def _(here):
        value = centers[here, :].astype(f32)
        high, low = split(value * value)
        center_sq[:, here] = dot(ones, high, NT) + dot(ones, low, NT)

    for stage in range(3, 7):
        sum_x.run(stage)

    sum_p = Pair(
        place,
        two(predicted, mine),
        two(predicted, other),
        two(predicted_sum, other),
        bufs[BUFS : 2 * BUFS],
        (send_p, recv_p),
    )
    sum_g = Sum(place, gradient, gradient, gradient_sum, EXTRA, bufs[2 * BUFS :], (send_g, recv_g))

    def laplace(left_sq, right_sq, inner):
        squared = left_sq + right_sq - 2.0 * inner
        return jnp.exp(jnp.sqrt(jnp.maximum(squared, floor_sq)) * (-1.0 / length_scale))

    def predict(index, between_them):
        here = pl.ds(pl.multiple_of(index * pair, pair), pair)
        value = arrived[pl.ds(index * 2, 2)].reshape(pair, width)
        value_sq = jnp.sum(value * value, axis=1, keepdims=True)
        batch_sq[here, :] = jnp.broadcast_to(value_sq, (pair, LANES))
        batch[here, :] = value.astype(bf16)

        @tiles(count, row_tile)
        def _(columns):
            inner = dot(batch[here, :], centers[columns, :], NT)
            high, low = split(laplace(batch_sq[here, 0:1], center_sq[0:1, columns], inner))
            kernel[:pair, columns] = high
            kernel[pair:, columns] = low

        both = dot(kernel[...], right_high[width:, :], NT)
        value = both[:pair] + (both[pair:] + dot(kernel[:pair, :], right_low[width:, :], NT))
        for k in range(2):
            columns = pl.ds(pl.multiple_of((index * 2 + k) * eigs, eigs), eigs)
            gradient[:, :, :, columns] = value[k * rows : (k + 1) * rows].reshape(block[1:-1] + (eigs,))

        between_them()
        for step in range(width // out_tile):
            here = slice(step * out_tile, (step + 1) * out_tile)
            both = dot(right_high[here, :], kernel[...], NT)
            value = both[:, :pair] + (both[:, pair:] + dot(right_low[here, :], kernel[:pair, :], NT))
            for j in range(out_tile // LANES):
                columns = slice(step * out_tile + j * LANES, step * out_tile + (j + 1) * LANES)
                for k in range(2):
                    piece = value[j * LANES : (j + 1) * LANES, k * rows : (k + 1) * rows]
                    predicted[index * 2 + k, :, :, :, columns] = piece.reshape(block[1:-1] + (rows,))

    def send_extra():
        pl.when(core == 1)(sum_g.core.start)

    def extra(stage):
        pl.when(core == 0)(functools.partial(sum_g.run, stage))

    predict(mine, lambda: None)
    sum_p.start_core()
    for k in range(2):
        sum_x.back[k].wait_recv()
    predict(other, send_extra)
    sum_p.run(0)
    extra(0)
    sum_x.finish()
    sum_x.finish_last()

    total = STEPS * rows
    value = batch[...].astype(f32)
    high, low = split(value * value)
    points_sq = (dot(ones, high, NT) + dot(ones, low, NT))[0:1, :]

    @tiles(total, rows)
    def _(here):
        inner = dot(batch[here, :], batch[...], NT)
        between[here, :] = laplace(batch_sq[here, 0:1], points_sq, inner)

    for stage in range(1, 7):
        sum_p.run(stage)
        extra(stage)

    pl.when(core == 1)(sum_g.back.wait_recv)
    targets_in.wait()
    projection = gradient_sum[...].reshape(rows, width)
    scale = step_size * weights[...]
    plain, weighted = [], []
    for step in range(STEPS):
        value = projection[:, step * eigs : (step + 1) * eigs]
        plain.append(split(value))
        weighted.append(split(value * scale))
    for step in range(STEPS):
        now = slice(step * rows, (step + 1) * rows)

        @tiles(count, row_tile)
        def _(here, now=now, step=step):
            value = dot3(weighted[step], (right_high[width:, here], right_low[width:, here]))
            value = value - jnp.where(is_owned(now, rows, here.start, row_tile), step_size, 0.0)
            update_high[now, here], update_low[now, here] = split(value)

        for past in range(step):
            then = slice(past * rows, (past + 1) * rows)
            value = dot3(weighted[step], plain[past], NT) - step_size * between[now, then]
            effect_high[now, then], effect_low[now, then] = split(value)
    sum_p.finish()
    for k in range(2):
        sum_p.back[k].wait_recv()
    for step in range(STEPS):
        now, then = slice(step * rows, (step + 1) * rows), slice(0, step * rows)
        pieces = [
            predicted_sum[step, :, :, :, j * LANES : (j + 1) * LANES].reshape(rows, rows)
            for j in range(width // LANES)
        ]
        value = jnp.concatenate(pieces, axis=0) - targets[step]
        if step > 0:
            value = value + dot3(
                (residual_high[:, then], residual_low[:, then]), (effect_high[now, then], effect_low[now, then]), NT
            )
        residual[step] = value[:outputs]
        if step < STEPS - 1:
            residual_high[:, now], residual_low[:, now] = split(value)

    sum_p.finish_last()
    pl.when(core == 1)(sum_g.core.wait_send)
    pl.when(core == 0)(sum_g.finish)


def update_kernel(update_high, update_low, coefs, residual, new_coefs, residuals, high, low):
    step = pl.program_id(0)

    @pl.when(step == 0)
    def _():
        high[...], low[...] = split(jnp.concatenate([residual[step] for step in range(STEPS)], axis=1))

    residuals[0] = residual[step]
    new_coefs[...] = coefs[...] + dot3((high[...], low[...]), (update_high[...], update_low[...]))


def body(sizes, centers, coefs, eigvecs, eig_weights, landmark_index, batch_index, targets):
    count, width = centers.shape
    outputs = coefs.shape[1]
    eigs = eigvecs.shape[1]
    rows = batch_index.shape[1]
    total = STEPS * rows
    block = (sizes["x"], sizes["y"], 8, width)
    bufs = pair_scratch(sizes, block) * 2 + sum_scratch(sizes, EXTRA, block)
    dma = pltpu.SemaphoreType.DMA
    vmem = pl.BlockSpec(memory_space=pltpu.VMEM)
    hbm = pl.BlockSpec(memory_space=pl.ANY)
    residual, update_high, update_low = pl.pallas_call(
        functools.partial(main_kernel, sizes),
        out_shape=[
            jax.ShapeDtypeStruct((STEPS, outputs, rows), f32),
            jax.ShapeDtypeStruct((total, count), bf16),
            jax.ShapeDtypeStruct((total, count), bf16),
        ],
        in_specs=[vmem, hbm, vmem, vmem, vmem, vmem, hbm],
        out_specs=[vmem] * 3,
        scratch_shapes=[
            pltpu.VMEM((width, count), f32),
            pltpu.VMEM((STEPS, width, rows), f32),
            pltpu.VMEM((width + eigs, count), bf16),
            pltpu.VMEM((width + eigs, count), bf16),
            pltpu.VMEM((8, count), f32),
            pltpu.VMEM((STEPS,) + block, f32),
            pltpu.VMEM((STEPS,) + block, f32),
            pltpu.VMEM((total, LANES), jnp.int32),
            pltpu.VMEM((total, width), bf16),
            pltpu.VMEM((4 * rows, count), bf16),
            pltpu.VMEM((total, LANES), f32),
            pltpu.VMEM((total, total), f32),
            pltpu.VMEM((STEPS,) + block, f32),
            pltpu.VMEM(block, f32),
            pltpu.VMEM((STEPS,) + block, f32),
            pltpu.VMEM(block, f32),
            pltpu.VMEM((total, total), bf16),
            pltpu.VMEM((total, total), bf16),
            pltpu.VMEM((width, total), bf16),
            pltpu.VMEM((width, total), bf16),
            dma((2,)),
            dma((24,)),
            dma((24,)),
            dma((24,)),
            dma((24,)),
            dma((8,)),
            dma((8,)),
        ]
        + bufs,
        compiler_params=pltpu.CompilerParams(
            collective_id=0, has_side_effects=True, vmem_limit_bytes=56 * MIB
        ),
        name="predict",
    )(
        centers,
        coefs.T,
        eigvecs,
        eig_weights.reshape(1, eigs),
        landmark_index.reshape(1, -1),
        batch_index,
        targets.transpose(0, 2, 1),
    )

    tile = count // STEPS
    new_coefs, residuals = pl.pallas_call(
        update_kernel,
        grid=(STEPS,),
        out_shape=[
            jax.ShapeDtypeStruct((outputs, count), f32),
            jax.ShapeDtypeStruct((STEPS, outputs, rows), f32),
        ],
        in_specs=[
            pl.BlockSpec((total, tile), lambda i: (0, i)),
            pl.BlockSpec((total, tile), lambda i: (0, i)),
            pl.BlockSpec((outputs, tile), lambda i: (0, i)),
            pl.BlockSpec((STEPS, outputs, rows), lambda i: (0, 0, 0)),
        ],
        out_specs=[
            pl.BlockSpec((outputs, tile), lambda i: (0, i)),
            pl.BlockSpec((1, outputs, rows), lambda i: (i, 0, 0)),
        ],
        scratch_shapes=[pltpu.VMEM((outputs, total), bf16)] * 2,
        compiler_params=pltpu.CompilerParams(vmem_limit_bytes=60 * MIB),
        name="update",
    )(update_high, update_low, coefs.T, residual)
    return new_coefs.T, residuals.transpose(0, 2, 1)


def solution(mesh, sizes=SIZES):
    in_specs = (
        P(("grp", "ctr"), None),
        P(("grp", "ctr"), None),
        P(("grp", "ctr"), None),
        P(),
        P(("grp", "ctr")),
        P(),
        P(),
    )
    out_specs = (P(("grp", "ctr"), None), P())
    return jax.shard_map(
        functools.partial(body, sizes),
        mesh=mesh,
        in_specs=in_specs,
        out_specs=out_specs,
        check_vma=False,
    )
```

```python
import functools

import jax
import jax.numpy as jnp
from jax import lax
from jax.experimental import pallas as pl
from jax.experimental.pallas import tpu as pltpu
from jax.sharding import PartitionSpec as P

STEPS = 4
LANES = 128
TILE = 256
MIB = 2**20
SIZES = {"x": 4, "y": 4, "z": 8}

floor_sq = 0.01
length_scale = 0.25
step_size = 0.5

MESH = pl.DeviceIdType.MESH
f32, bf16 = jnp.float32, jnp.bfloat16
NT = (((1,), (1,)), ((), ()))
NN = (((1,), (0,)), ((), ()))


def dot(left, right, dims=NN):
    return lax.dot_general(left, right, dims, preferred_element_type=f32)


def split(value):
    high = value.astype(bf16)
    return high, (value - high.astype(f32)).astype(bf16)


def dot3(left, right, dims=NN):
    return dot(left[0], right[0], dims) + (dot(left[0], right[1], dims) + dot(left[1], right[0], dims))


def span(index):
    return pl.ds(pl.multiple_of(index * LANES, LANES), LANES)


class Copies:
    def __init__(self, place, sems, index, like):
        self.send, self.recv = (sem.at[index] for sem in sems)
        self.like, self.copies = like, []
        self.device = place[2]

    def to(self, axis, by, src, dst):
        self.copies.append(self.copy(axis, by, src, dst))

    def copy(self, axis, by, src, dst):
        return pltpu.make_async_remote_copy(
            src_ref=src,
            dst_ref=dst,
            send_sem=self.send,
            recv_sem=self.recv,
            device_id=self.device(axis, by),
            device_id_type=MESH,
        )

    def start(self):
        for copy in self.copies:
            copy.start()

    def wait_recv(self):
        if self.copies:
            self.copy("c", 1, self.like, self.like).wait_recv()

    def wait_send(self):
        if self.copies:
            self.copy("c", 1, self.like, self.like).wait_send()


def add(terms, into):
    value = terms[0][...]
    for term in terms[1:]:
        value = value + term[...]
    into[...] = value


class Sum:
    def __init__(self, place, theirs, own, out, order, bufs, sems):
        sizes, me, device = place

        def along(ref, dims, axis, index):
            if axis == "z":
                return ref.at[(slice(None),) * (len(dims) + 1) + (span(index),)]
            return ref.at[tuple(index if dim == axis else slice(None) for dim in dims)]

        def region(fixed):
            return out.at[
                me["x"] if "x" in fixed else slice(None),
                me["y"] if "y" in fixed else slice(None),
                slice(None),
                span(me["z"]) if "z" in fixed else slice(None),
            ]

        self.core = Copies(place, sems, 0, bufs[0])
        self.core.to("c", 1, theirs, bufs[0])
        self.stages = []
        copies, terms, dims = self.core, [own, bufs[0]], "xy"
        for phase in range(3):
            axis = order[phase]
            total, landing = bufs[1 + 2 * phase], bufs[2 + 2 * phase]
            sends = Copies(place, sems, 1 + phase, landing)
            for by in range(1, sizes[axis]):
                index = lax.rem(me[axis] + by, sizes[axis])
                sends.to(axis, by, along(total, dims, axis, index), landing.at[by - 1])
            self.stages.append((copies, terms, total, sends))
            terms = [along(total, dims, axis, me[axis])] + [landing.at[by - 1] for by in range(1, sizes[axis])]
            copies, dims = sends, dims.replace(axis, "")
        total = region("xyz")
        for phase in range(3):
            axis = order[2 - phase]
            here = region(order[: 3 - phase])
            sends = Copies(place, sems, 4 + phase, bufs[6 - 2 * phase])
            for by in range(1, sizes[axis]):
                sends.to(axis, by, here, here)
            self.stages.append((copies, terms, total, sends))
            copies, terms, total = sends, None, None
        self.back = Copies(place, sems, 7, bufs[0])
        self.back.to("c", 1, out, out)
        self.stages.append((copies, None, None, self.back))

    def run(self, stage):
        copies, terms, total, sends = self.stages[stage]
        copies.wait_recv()
        if terms is not None:
            add(terms, total)
        sends.start()

    def finish(self):
        for stage in self.stages:
            stage[3].wait_send()


class Pair:
    def __init__(self, place, theirs, own, out, bufs, sems):
        sizes, me, device = place
        self.taken, self.total0, landing0, self.total1, landing1, self.total2, landing2 = bufs
        self.far = sorted(range(sizes["x"]), key=lambda by: -min(by, sizes["x"] - by))

        def first(ref, k, index):
            return ref.at[k, index] if k == 0 else ref.at[k, :, index]

        def to(axis, by):
            return lax.rem(me[axis] + by, sizes[axis])

        self.core, self.one, self.two, self.up2, self.up1, self.back = [], [], [], [], [], []
        self.terms1, self.terms2, self.sums = [], [], []
        for k in range(2):
            axis, other = ("x", "y") if k == 0 else ("y", "x")
            base, side = 11 * k, sizes[axis]
            core, up1 = {}, {}
            one = Copies(place, sems, base + 1, landing0.at[k])
            two = Copies(place, sems, base + 2, landing1.at[k])
            up2 = Copies(place, sems, base + 3, landing1.at[k])
            back = Copies(place, sems, base, self.taken.at[k])
            for by in range(side):
                core[by] = Copies(place, sems, base + 4 + by, landing0.at[k, 0])
                index = to(axis, by)
                core[by].to("c", 1, first(theirs, k, index), first(self.taken, k, index))
                here = first(out, k, index)
                back.to("c", 1, here, here)
            here = out.at[k, me["x"], me["y"]]
            for by in range(1, sizes[other]):
                two.to(other, by, self.total1.at[k, to(other, by)], landing1.at[k, by - 1])
                up2.to(other, by, here, here)
            here = first(out, k, me[axis])
            for by in range(1, sizes[axis]):
                one.to(axis, by, first(self.total0, k, to(axis, by)), landing0.at[k, by - 1])
                up1[by] = Copies(place, sems, base + 7 + by, landing0.at[k, 0])
                up1[by].to(axis, by, here, here)
            self.sums.append(
                [
                    [first(ref, k, to(axis, by)) for ref in (own, self.taken, self.total0)]
                    for by in range(side)
                ]
            )
            self.terms1.append(
                [first(self.total0, k, me[axis])] + [landing0.at[k, by - 1] for by in range(1, sizes[axis])]
            )
            self.terms2.append(
                [self.total1.at[k, me[other]]] + [landing1.at[k, by - 1] for by in range(1, sizes[other])]
            )
            self.core.append(core)
            self.one.append(one)
            self.two.append(two)
            self.up2.append(up2)
            self.up1.append(up1)
            self.back.append(back)
        self.down = Copies(place, sems, 22, landing2)
        self.up = Copies(place, sems, 23, landing2)
        self.mine = out.at[:, me["x"], me["y"], :, span(me["z"])]
        for by in range(1, sizes["z"]):
            self.down.to("z", by, self.total2.at[:, :, span(to("z", by))], landing2.at[by - 1])
            self.up.to("z", by, self.mine, self.mine)
        self.last = [self.total2.at[:, :, span(me["z"])]] + [landing2.at[by - 1] for by in range(1, sizes["z"])]

    def start_core(self):
        for by in self.far:
            for k in range(2):
                self.core[k][by].start()

    def run(self, stage):
        if stage == 0:
            for by in self.far:
                for k in range(2):
                    self.core[k][by].wait_recv()
                    own, taken, total = self.sums[k][by]
                    add([own, taken], total)
                    if by > 0:
                        self.one[k].copies[by - 1].start()
        if stage == 6:
            for by in reversed(self.far[:-1]):
                for k in range(2):
                    self.up1[k][by].wait_recv()
                    self.back[k].copies[len(self.far) - by].start()
        if stage == 3:
            self.down.wait_recv()
            add(self.last, self.mine)
            self.up.start()
        elif stage == 4:
            self.up.wait_recv()
        for k in range(2):
            if stage == 1:
                self.one[k].wait_recv()
                add(self.terms1[k], self.total1.at[k])
                self.two[k].start()
            elif stage == 2:
                self.two[k].wait_recv()
                add(self.terms2[k], self.total2.at[k])
            elif stage == 4:
                self.up2[k].start()
            elif stage == 5:
                self.up2[k].wait_recv()
                for by in self.far[:-1]:
                    self.up1[k][by].start()
                self.back[k].copies[0].start()
        if stage == 2:
            self.down.start()

    def finish(self):
        for core in self.core:
            for copies in core.values():
                copies.wait_send()
        for copies in self.one + self.two + [self.down, self.up] + self.up2:
            copies.wait_send()

    def finish_last(self):
        for up1 in self.up1:
            for copies in up1.values():
                copies.wait_send()
        for copies in self.back:
            copies.wait_send()


def sum_scratch(sizes, order, block):
    block = list(block)
    dims = "xy"
    scratch = [pltpu.VMEM(tuple(block), f32)] * 2
    for phase, axis in enumerate(order):
        if axis == "z":
            block[-1] = LANES
        else:
            block.pop(dims.index(axis))
            dims = dims.replace(axis, "")
        scratch.append(pltpu.VMEM((sizes[axis] - 1,) + tuple(block), f32))
        if phase < 2:
            scratch.append(pltpu.VMEM(tuple(block), f32))
    return scratch


def pair_scratch(sizes, block):
    side, deep, rows, width = block
    shapes = [
        (2,) + block,
        (2,) + block,
        (2, side - 1, side, rows, width),
        (2, side, rows, width),
        (2, side - 1, rows, width),
        (2, rows, width),
        (sizes["z"] - 1, 2, rows, LANES),
    ]
    return [pltpu.VMEM(shape, f32) for shape in shapes]


EXTRA = "zxy"
BUFS = 7


def main_kernel(
    sizes,
    centers_hbm,
    coefs_hbm,
    eigvecs_hbm,
    weights,
    landmarks,
    batch_index,
    targets_hbm,
    residual_hbm,
    update_high_hbm,
    update_low_hbm,
    centers,
    eigvecs,
    residual,
    update_high,
    update_low,
    coefs,
    targets,
    right_high,
    right_low,
    center_sq,
    picked,
    arrived,
    points,
    batch,
    kernel,
    batch_sq,
    between,
    predicted,
    gradient,
    predicted_sum,
    gradient_sum,
    effect_high,
    effect_low,
    residual_high,
    residual_low,
    local_sem,
    send_x,
    recv_x,
    send_p,
    recv_p,
    send_g,
    recv_g,
    *bufs,
):
    grp, ctr = lax.axis_index("grp"), lax.axis_index("ctr")
    core, y = lax.rem(grp, 2), lax.div(grp, 2)
    z, x = lax.div(ctr, sizes["x"]), lax.rem(ctr, sizes["x"])
    me = {"x": x, "y": y, "z": z}

    def device(axis, by):
        if axis == "c":
            return (y * 2 + 1 - core, ctr)
        to = lax.rem(me[axis] + by, sizes[axis])
        if axis == "x":
            return (grp, z * sizes["x"] + to)
        if axis == "y":
            return (to * 2 + core, ctr)
        return (grp, to * sizes["x"] + x)

    place = (sizes, me, device)
    peers = [("c", 1)] + [(axis, by) for axis in "xyz" for by in range(1, sizes[axis])]
    barrier = pltpu.get_barrier_semaphore()
    for axis, by in peers:
        pl.semaphore_signal(barrier, inc=1, device_id=device(axis, by), device_id_type=MESH)

    count, width = centers.shape
    outputs = coefs_hbm.shape[0]
    eigs = eigvecs.shape[1]
    rows = batch_index.shape[1]
    coefs_in = pltpu.make_async_copy(coefs_hbm, coefs.at[:outputs], local_sem.at[0])
    targets_in = pltpu.make_async_copy(targets_hbm, targets.at[:, :outputs], local_sem.at[1])
    centers_in = pltpu.make_async_copy(centers_hbm, centers, local_sem.at[2])
    eigvecs_in = pltpu.make_async_copy(eigvecs_hbm, eigvecs, local_sem.at[3])
    updates_out = [
        pltpu.make_async_copy(update_high, update_high_hbm, local_sem.at[4]),
        pltpu.make_async_copy(update_low, update_low_hbm, local_sem.at[5]),
    ]
    residuals_out = [
        pltpu.make_async_copy(residual.at[step], residual_hbm.at[step], local_sem.at[6 + step])
        for step in range(STEPS)
    ]
    centers_in.start()
    coefs_in.start()
    eigvecs_in.start()
    targets_in.start()
    coefs[outputs:, :] = jnp.zeros((width - outputs, count), f32)
    targets[:, outputs:, :] = jnp.zeros((STEPS, width - outputs, rows), f32)
    pair = 2 * rows
    block = (2,) + tuple(picked.shape[1:])
    row_tile, tile, out_tile = min(TILE, count), min(TILE, width), max(width // 2, LANES)
    offset = (grp * lax.axis_size("ctr") + ctr) * count

    def tiles(length, size):
        def loop(step):
            @pl.loop(0, length // size)
            def _(index):
                step(pl.ds(pl.multiple_of(index * size, size), size))

        return loop

    for step in range(STEPS):
        local = jnp.broadcast_to(batch_index[step : step + 1, :] - offset, (LANES, rows))
        points[step * rows : (step + 1) * rows, :] = local.T

    def is_owned(here, length, start, size):
        local = points[here, 0:1] - start
        return local == lax.broadcasted_iota(jnp.int32, (length, size), 1)

    def pick(index):
        owned = is_owned(pl.ds(pl.multiple_of(index * pair, pair), pair), pair, 0, count)
        owned = jnp.where(owned, 1.0, 0.0).astype(bf16)

        @tiles(width, tile)
        def _(columns):
            value = dot(owned, centers[:, columns])
            picked[pl.ds(index * 2, 2), :, :, :, columns] = value.reshape(block[:-1] + (tile,))

    mine, other = core, 1 - core
    def two(ref, index):
        return ref.at[pl.ds(index * 2, 2)]

    sum_x = Pair(place, two(picked, other), two(picked, mine), two(arrived, mine), bufs[:BUFS], (send_x, recv_x))
    centers_in.wait()
    pick(other)
    pl.semaphore_wait(barrier, len(peers))
    sum_x.start_core()
    pick(mine)
    sum_x.run(0)

    coefs_in.wait()

    @tiles(width, tile // 2)
    def _(here):
        right_high[here, :], right_low[here, :] = split(coefs[here, :])

    sum_x.run(1)

    eigvecs_in.wait()
    eig_high, eig_low = split(eigvecs[...].T)

    @tiles(count, row_tile)
    def _(here):
        local = landmarks[...] - offset - here.start
        at = jnp.where(
            local == lax.broadcasted_iota(jnp.int32, (row_tile, landmarks.shape[1]), 0), 1.0, 0.0
        ).astype(bf16)
        right_high[width:, here] = dot(eig_high, at, NT).astype(bf16)
        right_low[width:, here] = dot(eig_low, at, NT).astype(bf16)

    sum_x.run(2)
    ones = jnp.ones((8, width), bf16)

    @tiles(count, row_tile)
    def _(here):
        value = centers[here, :].astype(f32)
        high, low = split(value * value)
        center_sq[:, here] = dot(ones, high, NT) + dot(ones, low, NT)

    for stage in range(3, 7):
        sum_x.run(stage)

    sum_p = Pair(
        place,
        two(predicted, mine),
        two(predicted, other),
        two(predicted_sum, other),
        bufs[BUFS : 2 * BUFS],
        (send_p, recv_p),
    )
    sum_g = Sum(place, gradient, gradient, gradient_sum, EXTRA, bufs[2 * BUFS :], (send_g, recv_g))

    def laplace(left_sq, right_sq, inner):
        squared = left_sq + right_sq - 2.0 * inner
        return jnp.exp(jnp.sqrt(jnp.maximum(squared, floor_sq)) * (-1.0 / length_scale))

    def predict(index, between_them):
        here = pl.ds(pl.multiple_of(index * pair, pair), pair)
        value = arrived[pl.ds(index * 2, 2)].reshape(pair, width)
        value_sq = jnp.sum(value * value, axis=1, keepdims=True)
        batch_sq[here, :] = jnp.broadcast_to(value_sq, (pair, LANES))
        batch[here, :] = value.astype(bf16)

        @tiles(count, row_tile)
        def _(columns):
            inner = dot(batch[here, :], centers[columns, :], NT)
            high, low = split(laplace(batch_sq[here, 0:1], center_sq[0:1, columns], inner))
            kernel[:pair, columns] = high
            kernel[pair:, columns] = low

        both = dot(kernel[...], right_high[width:, :], NT)
        value = both[:pair] + (both[pair:] + dot(kernel[:pair, :], right_low[width:, :], NT))
        for k in range(2):
            columns = pl.ds(pl.multiple_of((index * 2 + k) * eigs, eigs), eigs)
            gradient[:, :, :, columns] = value[k * rows : (k + 1) * rows].reshape(block[1:-1] + (eigs,))

        between_them()
        for step in range(width // out_tile):
            here = slice(step * out_tile, (step + 1) * out_tile)
            both = dot(right_high[here, :], kernel[...], NT)
            value = both[:, :pair] + (both[:, pair:] + dot(right_low[here, :], kernel[:pair, :], NT))
            for j in range(out_tile // LANES):
                columns = slice(step * out_tile + j * LANES, step * out_tile + (j + 1) * LANES)
                for k in range(2):
                    piece = value[j * LANES : (j + 1) * LANES, k * rows : (k + 1) * rows]
                    predicted[index * 2 + k, :, :, :, columns] = piece.reshape(block[1:-1] + (rows,))

    def send_extra():
        pl.when(core == 1)(sum_g.core.start)

    def extra(stage):
        pl.when(core == 0)(functools.partial(sum_g.run, stage))

    predict(mine, lambda: None)
    sum_p.start_core()
    for k in range(2):
        sum_x.back[k].wait_recv()
    predict(other, send_extra)
    sum_p.run(0)
    extra(0)
    sum_x.finish()
    sum_x.finish_last()

    total = STEPS * rows
    value = batch[...].astype(f32)
    high, low = split(value * value)
    points_sq = (dot(ones, high, NT) + dot(ones, low, NT))[0:1, :]

    @tiles(total, rows)
    def _(here):
        inner = dot(batch[here, :], batch[...], NT)
        between[here, :] = laplace(batch_sq[here, 0:1], points_sq, inner)

    for stage in range(1, 7):
        sum_p.run(stage)
        extra(stage)

    pl.when(core == 1)(sum_g.back.wait_recv)
    targets_in.wait()
    projection = gradient_sum[...].reshape(rows, width)
    scale = step_size * weights[...]
    plain, weighted = [], []
    for step in range(STEPS):
        value = projection[:, step * eigs : (step + 1) * eigs]
        plain.append(split(value))
        weighted.append(split(value * scale))
    for step in range(STEPS):
        now = slice(step * rows, (step + 1) * rows)

        @tiles(count, row_tile)
        def _(here, now=now, step=step):
            value = dot3(weighted[step], (right_high[width:, here], right_low[width:, here]))
            value = value - jnp.where(is_owned(now, rows, here.start, row_tile), step_size, 0.0)
            update_high[now, here], update_low[now, here] = split(value)

        for past in range(step):
            then = slice(past * rows, (past + 1) * rows)
            value = dot3(weighted[step], plain[past], NT) - step_size * between[now, then]
            effect_high[now, then], effect_low[now, then] = split(value)
    for copy in updates_out:
        copy.start()
    sum_p.finish()
    for k in range(2):
        sum_p.back[k].wait_recv()
    for step in range(STEPS):
        now, then = slice(step * rows, (step + 1) * rows), slice(0, step * rows)
        pieces = [
            predicted_sum[step, :, :, :, j * LANES : (j + 1) * LANES].reshape(rows, rows)
            for j in range(width // LANES)
        ]
        value = jnp.concatenate(pieces, axis=0) - targets[step]
        if step > 0:
            value = value + dot3(
                (residual_high[:, then], residual_low[:, then]), (effect_high[now, then], effect_low[now, then]), NT
            )
        residual[step] = value[:outputs]
        residuals_out[step].start()
        if step < STEPS - 1:
            residual_high[:, now], residual_low[:, now] = split(value)

    sum_p.finish_last()
    for copy in updates_out + residuals_out:
        copy.wait()
    pl.when(core == 1)(sum_g.core.wait_send)
    pl.when(core == 0)(sum_g.finish)


def update_kernel(update_high, update_low, coefs, residual, new_coefs, residuals, high, low):
    step = pl.program_id(0)

    @pl.when(step == 0)
    def _():
        high[...], low[...] = split(jnp.concatenate([residual[step] for step in range(STEPS)], axis=1))

    residuals[0] = residual[step]
    new_coefs[...] = coefs[...] + dot3((high[...], low[...]), (update_high[...], update_low[...]))


def body(sizes, centers, coefs, eigvecs, eig_weights, landmark_index, batch_index, targets):
    count, width = centers.shape
    outputs = coefs.shape[1]
    eigs = eigvecs.shape[1]
    rows = batch_index.shape[1]
    total = STEPS * rows
    block = (sizes["x"], sizes["y"], 8, width)
    bufs = pair_scratch(sizes, block) * 2 + sum_scratch(sizes, EXTRA, block)
    dma = pltpu.SemaphoreType.DMA
    vmem = pl.BlockSpec(memory_space=pltpu.VMEM)
    hbm = pl.BlockSpec(memory_space=pl.ANY)
    residual, update_high, update_low = pl.pallas_call(
        functools.partial(main_kernel, sizes),
        out_shape=[
            jax.ShapeDtypeStruct((STEPS, outputs, rows), f32),
            jax.ShapeDtypeStruct((total, count), bf16),
            jax.ShapeDtypeStruct((total, count), bf16),
        ],
        in_specs=[hbm, hbm, hbm, vmem, vmem, vmem, hbm],
        out_specs=[hbm] * 3,
        scratch_shapes=[
            pltpu.VMEM((count, width), bf16),
            pltpu.VMEM(eigvecs.shape, f32),
            pltpu.VMEM((STEPS, outputs, rows), f32),
            pltpu.VMEM((total, count), bf16),
            pltpu.VMEM((total, count), bf16),
            pltpu.VMEM((width, count), f32),
            pltpu.VMEM((STEPS, width, rows), f32),
            pltpu.VMEM((width + eigs, count), bf16),
            pltpu.VMEM((width + eigs, count), bf16),
            pltpu.VMEM((8, count), f32),
            pltpu.VMEM((STEPS,) + block, f32),
            pltpu.VMEM((STEPS,) + block, f32),
            pltpu.VMEM((total, LANES), jnp.int32),
            pltpu.VMEM((total, width), bf16),
            pltpu.VMEM((4 * rows, count), bf16),
            pltpu.VMEM((total, LANES), f32),
            pltpu.VMEM((total, total), f32),
            pltpu.VMEM((STEPS,) + block, f32),
            pltpu.VMEM(block, f32),
            pltpu.VMEM((STEPS,) + block, f32),
            pltpu.VMEM(block, f32),
            pltpu.VMEM((total, total), bf16),
            pltpu.VMEM((total, total), bf16),
            pltpu.VMEM((width, total), bf16),
            pltpu.VMEM((width, total), bf16),
            dma((6 + STEPS,)),
            dma((24,)),
            dma((24,)),
            dma((24,)),
            dma((24,)),
            dma((8,)),
            dma((8,)),
        ]
        + bufs,
        compiler_params=pltpu.CompilerParams(
            collective_id=0, has_side_effects=True, vmem_limit_bytes=56 * MIB
        ),
        name="predict",
    )(
        centers,
        coefs.T,
        eigvecs,
        eig_weights.reshape(1, eigs),
        landmark_index.reshape(1, -1),
        batch_index,
        targets.transpose(0, 2, 1),
    )

    tile = count // STEPS
    new_coefs, residuals = pl.pallas_call(
        update_kernel,
        grid=(STEPS,),
        out_shape=[
            jax.ShapeDtypeStruct((outputs, count), f32),
            jax.ShapeDtypeStruct((STEPS, outputs, rows), f32),
        ],
        in_specs=[
            pl.BlockSpec((total, tile), lambda i: (0, i)),
            pl.BlockSpec((total, tile), lambda i: (0, i)),
            pl.BlockSpec((outputs, tile), lambda i: (0, i)),
            pl.BlockSpec((STEPS, outputs, rows), lambda i: (0, 0, 0)),
        ],
        out_specs=[
            pl.BlockSpec((outputs, tile), lambda i: (0, i)),
            pl.BlockSpec((1, outputs, rows), lambda i: (i, 0, 0)),
        ],
        scratch_shapes=[pltpu.VMEM((outputs, total), bf16)] * 2,
        compiler_params=pltpu.CompilerParams(vmem_limit_bytes=60 * MIB),
        name="update",
    )(update_high, update_low, coefs.T, residual)
    return new_coefs.T, residuals.transpose(0, 2, 1)


def solution(mesh, sizes=SIZES):
    in_specs = (
        P(("grp", "ctr"), None),
        P(("grp", "ctr"), None),
        P(("grp", "ctr"), None),
        P(),
        P(("grp", "ctr")),
        P(),
        P(),
    )
    out_specs = (P(("grp", "ctr"), None), P())
    return jax.shard_map(
        functools.partial(body, sizes),
        mesh=mesh,
        in_specs=in_specs,
        out_specs=out_specs,
        check_vma=False,
    )
```

```python
import functools

import jax
import jax.numpy as jnp
from jax import lax
from jax.experimental import pallas as pl
from jax.experimental.pallas import tpu as pltpu
from jax.sharding import PartitionSpec as P

STEPS = 4
LANES = 128
TILE = 256
MIB = 2**20
SIZES = {"x": 4, "y": 4, "z": 8}

floor_sq = 0.01
length_scale = 0.25
step_size = 0.5

MESH = pl.DeviceIdType.MESH
f32, bf16 = jnp.float32, jnp.bfloat16
NT = (((1,), (1,)), ((), ()))
NN = (((1,), (0,)), ((), ()))


def dot(left, right, dims=NN):
    return lax.dot_general(left, right, dims, preferred_element_type=f32)


def split(value):
    high = value.astype(bf16)
    return high, (value - high.astype(f32)).astype(bf16)


def dot3(left, right, dims=NN):
    return dot(left[0], right[0], dims) + (dot(left[0], right[1], dims) + dot(left[1], right[0], dims))


def span(index):
    return pl.ds(pl.multiple_of(index * LANES, LANES), LANES)


class Copies:
    def __init__(self, place, sems, index, like):
        self.send, self.recv = (sem.at[index] for sem in sems)
        self.like, self.copies = like, []
        self.device = place[2]

    def to(self, axis, by, src, dst):
        self.copies.append(self.copy(axis, by, src, dst))

    def copy(self, axis, by, src, dst):
        return pltpu.make_async_remote_copy(
            src_ref=src,
            dst_ref=dst,
            send_sem=self.send,
            recv_sem=self.recv,
            device_id=self.device(axis, by),
            device_id_type=MESH,
        )

    def start(self):
        for copy in self.copies:
            copy.start()

    def wait_recv(self):
        if self.copies:
            self.copy("c", 1, self.like, self.like).wait_recv()

    def wait_send(self):
        if self.copies:
            self.copy("c", 1, self.like, self.like).wait_send()


def add(terms, into):
    value = terms[0][...]
    for term in terms[1:]:
        value = value + term[...]
    into[...] = value


class Sum:
    def __init__(self, place, theirs, own, out, order, bufs, sems):
        sizes, me, device = place

        def along(ref, dims, axis, index):
            if axis == "z":
                return ref.at[(slice(None),) * (len(dims) + 1) + (span(index),)]
            return ref.at[tuple(index if dim == axis else slice(None) for dim in dims)]

        def region(fixed):
            return out.at[
                me["x"] if "x" in fixed else slice(None),
                me["y"] if "y" in fixed else slice(None),
                slice(None),
                span(me["z"]) if "z" in fixed else slice(None),
            ]

        self.core = Copies(place, sems, 0, bufs[0])
        self.core.to("c", 1, theirs, bufs[0])
        self.stages = []
        copies, terms, dims = self.core, [own, bufs[0]], "xy"
        for phase in range(3):
            axis = order[phase]
            total, landing = bufs[1 + 2 * phase], bufs[2 + 2 * phase]
            sends = Copies(place, sems, 1 + phase, landing)
            for by in range(1, sizes[axis]):
                index = lax.rem(me[axis] + by, sizes[axis])
                sends.to(axis, by, along(total, dims, axis, index), landing.at[by - 1])
            self.stages.append((copies, terms, total, sends))
            terms = [along(total, dims, axis, me[axis])] + [landing.at[by - 1] for by in range(1, sizes[axis])]
            copies, dims = sends, dims.replace(axis, "")
        total = region("xyz")
        for phase in range(3):
            axis = order[2 - phase]
            here = region(order[: 3 - phase])
            sends = Copies(place, sems, 4 + phase, bufs[6 - 2 * phase])
            for by in range(1, sizes[axis]):
                sends.to(axis, by, here, here)
            self.stages.append((copies, terms, total, sends))
            copies, terms, total = sends, None, None
        self.back = Copies(place, sems, 7, bufs[0])
        self.back.to("c", 1, out, out)
        self.stages.append((copies, None, None, self.back))

    def run(self, stage):
        copies, terms, total, sends = self.stages[stage]
        copies.wait_recv()
        if terms is not None:
            add(terms, total)
        sends.start()

    def finish(self):
        for stage in self.stages:
            stage[3].wait_send()


class Pair:
    def __init__(self, place, theirs, own, out, bufs, sems):
        sizes, me, device = place
        self.taken, self.total0, landing0, self.total1, landing1, self.total2, landing2 = bufs
        self.far = sorted(range(sizes["x"]), key=lambda by: -min(by, sizes["x"] - by))

        def first(ref, k, index):
            return ref.at[k, index] if k == 0 else ref.at[k, :, index]

        def to(axis, by):
            return lax.rem(me[axis] + by, sizes[axis])

        self.core, self.one, self.two, self.up2, self.up1, self.back = [], [], [], [], [], []
        self.terms1, self.terms2, self.sums = [], [], []
        for k in range(2):
            axis, other = ("x", "y") if k == 0 else ("y", "x")
            base, side = 11 * k, sizes[axis]
            core, up1 = {}, {}
            one = Copies(place, sems, base + 1, landing0.at[k])
            two = Copies(place, sems, base + 2, landing1.at[k])
            up2 = Copies(place, sems, base + 3, landing1.at[k])
            back = Copies(place, sems, base, self.taken.at[k])
            for by in range(side):
                core[by] = Copies(place, sems, base + 4 + by, landing0.at[k, 0])
                index = to(axis, by)
                core[by].to("c", 1, first(theirs, k, index), first(self.taken, k, index))
                here = first(out, k, index)
                back.to("c", 1, here, here)
            here = out.at[k, me["x"], me["y"]]
            for by in range(1, sizes[other]):
                two.to(other, by, self.total1.at[k, to(other, by)], landing1.at[k, by - 1])
                up2.to(other, by, here, here)
            here = first(out, k, me[axis])
            for by in range(1, sizes[axis]):
                one.to(axis, by, first(self.total0, k, to(axis, by)), landing0.at[k, by - 1])
                up1[by] = Copies(place, sems, base + 7 + by, landing0.at[k, 0])
                up1[by].to(axis, by, here, here)
            self.sums.append(
                [
                    [first(ref, k, to(axis, by)) for ref in (own, self.taken, self.total0)]
                    for by in range(side)
                ]
            )
            self.terms1.append(
                [first(self.total0, k, me[axis])] + [landing0.at[k, by - 1] for by in range(1, sizes[axis])]
            )
            self.terms2.append(
                [self.total1.at[k, me[other]]] + [landing1.at[k, by - 1] for by in range(1, sizes[other])]
            )
            self.core.append(core)
            self.one.append(one)
            self.two.append(two)
            self.up2.append(up2)
            self.up1.append(up1)
            self.back.append(back)
        self.down = Copies(place, sems, 22, landing2)
        self.up = Copies(place, sems, 23, landing2)
        self.mine = out.at[:, me["x"], me["y"], :, span(me["z"])]
        for by in range(1, sizes["z"]):
            self.down.to("z", by, self.total2.at[:, :, span(to("z", by))], landing2.at[by - 1])
            self.up.to("z", by, self.mine, self.mine)
        self.last = [self.total2.at[:, :, span(me["z"])]] + [landing2.at[by - 1] for by in range(1, sizes["z"])]

    def start_core(self):
        for by in self.far:
            for k in range(2):
                self.core[k][by].start()

    def run(self, stage):
        if stage == 0:
            for by in self.far:
                for k in range(2):
                    self.core[k][by].wait_recv()
                    own, taken, total = self.sums[k][by]
                    add([own, taken], total)
                    if by > 0:
                        self.one[k].copies[by - 1].start()
        if stage == 6:
            for by in reversed(self.far[:-1]):
                for k in range(2):
                    self.up1[k][by].wait_recv()
                    self.back[k].copies[len(self.far) - by].start()
        if stage == 3:
            self.down.wait_recv()
            add(self.last, self.mine)
            self.up.start()
        elif stage == 4:
            self.up.wait_recv()
        for k in range(2):
            if stage == 1:
                self.one[k].wait_recv()
                add(self.terms1[k], self.total1.at[k])
                self.two[k].start()
            elif stage == 2:
                self.two[k].wait_recv()
                add(self.terms2[k], self.total2.at[k])
            elif stage == 4:
                self.up2[k].start()
            elif stage == 5:
                self.up2[k].wait_recv()
                for by in self.far[:-1]:
                    self.up1[k][by].start()
                self.back[k].copies[0].start()
        if stage == 2:
            self.down.start()

    def finish(self):
        for core in self.core:
            for copies in core.values():
                copies.wait_send()
        for copies in self.one + self.two + [self.down, self.up] + self.up2:
            copies.wait_send()

    def finish_last(self):
        for up1 in self.up1:
            for copies in up1.values():
                copies.wait_send()
        for copies in self.back:
            copies.wait_send()


def sum_scratch(sizes, order, block):
    block = list(block)
    dims = "xy"
    scratch = [pltpu.VMEM(tuple(block), f32)] * 2
    for phase, axis in enumerate(order):
        if axis == "z":
            block[-1] = LANES
        else:
            block.pop(dims.index(axis))
            dims = dims.replace(axis, "")
        scratch.append(pltpu.VMEM((sizes[axis] - 1,) + tuple(block), f32))
        if phase < 2:
            scratch.append(pltpu.VMEM(tuple(block), f32))
    return scratch


def pair_scratch(sizes, block):
    side, deep, rows, width = block
    shapes = [
        (2,) + block,
        (2,) + block,
        (2, side - 1, side, rows, width),
        (2, side, rows, width),
        (2, side - 1, rows, width),
        (2, rows, width),
        (sizes["z"] - 1, 2, rows, LANES),
    ]
    return [pltpu.VMEM(shape, f32) for shape in shapes]


EXTRA = "zxy"
BUFS = 7


def main_kernel(
    sizes,
    centers_hbm,
    coefs_hbm,
    eigvecs_hbm,
    weights,
    landmarks,
    batch_index,
    targets_hbm,
    residual_hbm,
    update_high_hbm,
    update_low_hbm,
    centers,
    eigvecs,
    residual,
    update_high,
    update_low,
    coefs,
    targets,
    right_high,
    right_low,
    center_sq,
    picked,
    arrived,
    points,
    batch,
    kernel,
    batch_sq,
    between,
    predicted,
    gradient,
    predicted_sum,
    gradient_sum,
    effect_high,
    effect_low,
    residual_high,
    residual_low,
    local_sem,
    send_x,
    recv_x,
    send_p,
    recv_p,
    send_g,
    recv_g,
    *bufs,
):
    grp, ctr = lax.axis_index("grp"), lax.axis_index("ctr")
    core, y = lax.rem(grp, 2), lax.div(grp, 2)
    z, x = lax.div(ctr, sizes["x"]), lax.rem(ctr, sizes["x"])
    me = {"x": x, "y": y, "z": z}

    def device(axis, by):
        if axis == "c":
            return (y * 2 + 1 - core, ctr)
        to = lax.rem(me[axis] + by, sizes[axis])
        if axis == "x":
            return (grp, z * sizes["x"] + to)
        if axis == "y":
            return (to * 2 + core, ctr)
        return (grp, to * sizes["x"] + x)

    place = (sizes, me, device)
    peers = [("c", 1)] + [(axis, by) for axis in "xyz" for by in range(1, sizes[axis])]
    barrier = pltpu.get_barrier_semaphore()
    for axis, by in peers:
        pl.semaphore_signal(barrier, inc=1, device_id=device(axis, by), device_id_type=MESH)

    count, width = centers.shape
    outputs = coefs_hbm.shape[0]
    eigs = eigvecs.shape[1]
    rows = batch_index.shape[1]
    coefs_in = pltpu.make_async_copy(coefs_hbm, coefs.at[:outputs], local_sem.at[0])
    targets_in = pltpu.make_async_copy(targets_hbm, targets.at[:, :outputs], local_sem.at[1])
    centers_in = pltpu.make_async_copy(centers_hbm, centers, local_sem.at[2])
    eigvecs_in = pltpu.make_async_copy(eigvecs_hbm, eigvecs, local_sem.at[3])
    updates_out = [
        pltpu.make_async_copy(update_high, update_high_hbm, local_sem.at[4]),
        pltpu.make_async_copy(update_low, update_low_hbm, local_sem.at[5]),
    ]
    residuals_out = [
        pltpu.make_async_copy(residual.at[step], residual_hbm.at[step], local_sem.at[6 + step])
        for step in range(STEPS)
    ]
    centers_in.start()
    coefs_in.start()
    eigvecs_in.start()
    targets_in.start()
    coefs[outputs:, :] = jnp.zeros((width - outputs, count), f32)
    targets[:, outputs:, :] = jnp.zeros((STEPS, width - outputs, rows), f32)
    pair = 2 * rows
    block = (2,) + tuple(picked.shape[1:])
    row_tile, tile, out_tile = min(TILE, count), min(TILE, width), max(width // 2, LANES)
    offset = (grp * lax.axis_size("ctr") + ctr) * count

    def tiles(length, size):
        def loop(step):
            @pl.loop(0, length // size)
            def _(index):
                step(pl.ds(pl.multiple_of(index * size, size), size))

        return loop

    for step in range(STEPS):
        local = jnp.broadcast_to(batch_index[step : step + 1, :] - offset, (LANES, rows))
        points[step * rows : (step + 1) * rows, :] = local.T

    def is_owned(here, length, start, size):
        local = points[here, 0:1] - start
        return local == lax.broadcasted_iota(jnp.int32, (length, size), 1)

    def pick(index):
        owned = is_owned(pl.ds(pl.multiple_of(index * pair, pair), pair), pair, 0, count)
        owned = jnp.where(owned, 1.0, 0.0).astype(bf16)

        @tiles(width, tile)
        def _(columns):
            value = dot(owned, centers[:, columns])
            picked[pl.ds(index * 2, 2), :, :, :, columns] = value.reshape(block[:-1] + (tile,))

    mine, other = core, 1 - core
    def two(ref, index):
        return ref.at[pl.ds(index * 2, 2)]

    sum_x = Pair(place, two(picked, other), two(picked, mine), two(arrived, mine), bufs[:BUFS], (send_x, recv_x))
    centers_in.wait()
    pick(other)
    pl.semaphore_wait(barrier, len(peers))
    sum_x.start_core()
    pick(mine)
    sum_x.run(0)

    coefs_in.wait()

    @tiles(width, tile // 2)
    def _(here):
        right_high[here, :], right_low[here, :] = split(coefs[here, :])

    sum_x.run(1)

    eigvecs_in.wait()
    eig_high, eig_low = split(eigvecs[...].T)

    @tiles(count, row_tile)
    def _(here):
        local = landmarks[...] - offset - here.start
        at = jnp.where(
            local == lax.broadcasted_iota(jnp.int32, (row_tile, landmarks.shape[1]), 0), 1.0, 0.0
        ).astype(bf16)
        right_high[width:, here] = dot(eig_high, at, NT).astype(bf16)
        right_low[width:, here] = dot(eig_low, at, NT).astype(bf16)

    sum_x.run(2)
    ones = jnp.ones((8, width), bf16)

    @tiles(count, row_tile)
    def _(here):
        value = centers[here, :].astype(f32)
        high, low = split(value * value)
        center_sq[:, here] = dot(ones, high, NT) + dot(ones, low, NT)

    for stage in range(3, 7):
        sum_x.run(stage)

    sum_p = Pair(
        place,
        two(predicted, mine),
        two(predicted, other),
        two(predicted_sum, other),
        bufs[BUFS : 2 * BUFS],
        (send_p, recv_p),
    )
    sum_g = Sum(place, gradient, gradient, gradient_sum, EXTRA, bufs[2 * BUFS :], (send_g, recv_g))

    def laplace(left_sq, right_sq, inner):
        squared = left_sq + right_sq - 2.0 * inner
        return jnp.exp(jnp.sqrt(jnp.maximum(squared, floor_sq)) * (-1.0 / length_scale))

    def predict(index, between_them):
        here = pl.ds(pl.multiple_of(index * pair, pair), pair)
        value = arrived[pl.ds(index * 2, 2)].reshape(pair, width)
        value_sq = jnp.sum(value * value, axis=1, keepdims=True)
        batch_sq[here, :] = jnp.broadcast_to(value_sq, (pair, LANES))
        batch[here, :] = value.astype(bf16)

        @tiles(count, row_tile)
        def _(columns):
            inner = dot(batch[here, :], centers[columns, :], NT)
            high, low = split(laplace(batch_sq[here, 0:1], center_sq[0:1, columns], inner))
            kernel[:pair, columns] = high
            kernel[pair:, columns] = low

        both = dot(kernel[...], right_high[width:, :], NT)
        value = both[:pair] + (both[pair:] + dot(kernel[:pair, :], right_low[width:, :], NT))
        for k in range(2):
            columns = pl.ds(pl.multiple_of((index * 2 + k) * eigs, eigs), eigs)
            gradient[:, :, :, columns] = value[k * rows : (k + 1) * rows].reshape(block[1:-1] + (eigs,))

        between_them()
        for step in range(width // out_tile):
            here = slice(step * out_tile, (step + 1) * out_tile)
            both = dot(right_high[here, :], kernel[...], NT)
            value = both[:, :pair] + (both[:, pair:] + dot(right_low[here, :], kernel[:pair, :], NT))
            for j in range(out_tile // LANES):
                columns = slice(step * out_tile + j * LANES, step * out_tile + (j + 1) * LANES)
                for k in range(2):
                    piece = value[j * LANES : (j + 1) * LANES, k * rows : (k + 1) * rows]
                    predicted[index * 2 + k, :, :, :, columns] = piece.reshape(block[1:-1] + (rows,))

    def send_extra():
        pl.when(core == 1)(sum_g.core.start)

    def extra(stage):
        pl.when(core == 0)(functools.partial(sum_g.run, stage))

    predict(mine, lambda: None)
    sum_p.start_core()
    for k in range(2):
        sum_x.back[k].wait_recv()
    predict(other, send_extra)
    sum_p.run(0)
    extra(0)
    sum_x.finish()
    sum_x.finish_last()

    total = STEPS * rows
    value = batch[...].astype(f32)
    high, low = split(value * value)
    points_sq = (dot(ones, high, NT) + dot(ones, low, NT))[0:1, :]

    @tiles(total, rows)
    def _(here):
        inner = dot(batch[here, :], batch[...], NT)
        between[here, :] = laplace(batch_sq[here, 0:1], points_sq, inner)

    for stage in range(1, 7):
        sum_p.run(stage)
        extra(stage)

    pl.when(core == 1)(sum_g.back.wait_recv)
    targets_in.wait()
    projection = gradient_sum[...].reshape(rows, width)
    scale = step_size * weights[...]
    plain, weighted = [], []
    for step in range(STEPS):
        value = projection[:, step * eigs : (step + 1) * eigs]
        plain.append(split(value))
        weighted.append(split(value * scale))
    weighted_all = tuple(jnp.concatenate([value[i] for value in weighted], axis=0) for i in range(2))
    plain_all = tuple(jnp.concatenate([value[i] for value in plain], axis=0) for i in range(2))

    @tiles(count, row_tile)
    def _(here):
        value = dot3(weighted_all, (right_high[width:, here], right_low[width:, here]))
        value = value - jnp.where(is_owned(slice(0, total), total, here.start, row_tile), step_size, 0.0)
        update_high[:, here], update_low[:, here] = split(value)

    for step in range(1, STEPS):
        now, then = slice(step * rows, (step + 1) * rows), slice(0, step * rows)
        past = tuple(value[: step * rows] for value in plain_all)
        value = dot3(weighted[step], past, NT) - step_size * between[now, then]
        effect_high[now, then], effect_low[now, then] = split(value)
    for copy in updates_out:
        copy.start()
    sum_p.finish()
    for k in range(2):
        sum_p.back[k].wait_recv()
    for step in range(STEPS):
        now, then = slice(step * rows, (step + 1) * rows), slice(0, step * rows)
        pieces = [
            predicted_sum[step, :, :, :, j * LANES : (j + 1) * LANES].reshape(rows, rows)
            for j in range(width // LANES)
        ]
        value = jnp.concatenate(pieces, axis=0) - targets[step]
        if step > 0:
            value = value + dot3(
                (residual_high[:, then], residual_low[:, then]), (effect_high[now, then], effect_low[now, then]), NT
            )
        residual[step] = value[:outputs]
        residuals_out[step].start()
        if step < STEPS - 1:
            residual_high[:, now], residual_low[:, now] = split(value)

    sum_p.finish_last()
    for copy in updates_out + residuals_out:
        copy.wait()
    pl.when(core == 1)(sum_g.core.wait_send)
    pl.when(core == 0)(sum_g.finish)


def update_kernel(update_high, update_low, coefs, residual, new_coefs, residuals, high, low):
    step = pl.program_id(0)

    @pl.when(step == 0)
    def _():
        high[...], low[...] = split(jnp.concatenate([residual[step] for step in range(STEPS)], axis=1))

    residuals[0] = residual[step]
    new_coefs[...] = coefs[...] + dot3((high[...], low[...]), (update_high[...], update_low[...]))


def body(sizes, centers, coefs, eigvecs, eig_weights, landmark_index, batch_index, targets):
    count, width = centers.shape
    outputs = coefs.shape[1]
    eigs = eigvecs.shape[1]
    rows = batch_index.shape[1]
    total = STEPS * rows
    block = (sizes["x"], sizes["y"], 8, width)
    bufs = pair_scratch(sizes, block) * 2 + sum_scratch(sizes, EXTRA, block)
    dma = pltpu.SemaphoreType.DMA
    vmem = pl.BlockSpec(memory_space=pltpu.VMEM)
    hbm = pl.BlockSpec(memory_space=pl.ANY)
    residual, update_high, update_low = pl.pallas_call(
        functools.partial(main_kernel, sizes),
        out_shape=[
            jax.ShapeDtypeStruct((STEPS, outputs, rows), f32),
            jax.ShapeDtypeStruct((total, count), bf16),
            jax.ShapeDtypeStruct((total, count), bf16),
        ],
        in_specs=[hbm, hbm, hbm, vmem, vmem, vmem, hbm],
        out_specs=[hbm] * 3,
        scratch_shapes=[
            pltpu.VMEM((count, width), bf16),
            pltpu.VMEM(eigvecs.shape, f32),
            pltpu.VMEM((STEPS, outputs, rows), f32),
            pltpu.VMEM((total, count), bf16),
            pltpu.VMEM((total, count), bf16),
            pltpu.VMEM((width, count), f32),
            pltpu.VMEM((STEPS, width, rows), f32),
            pltpu.VMEM((width + eigs, count), bf16),
            pltpu.VMEM((width + eigs, count), bf16),
            pltpu.VMEM((8, count), f32),
            pltpu.VMEM((STEPS,) + block, f32),
            pltpu.VMEM((STEPS,) + block, f32),
            pltpu.VMEM((total, LANES), jnp.int32),
            pltpu.VMEM((total, width), bf16),
            pltpu.VMEM((4 * rows, count), bf16),
            pltpu.VMEM((total, LANES), f32),
            pltpu.VMEM((total, total), f32),
            pltpu.VMEM((STEPS,) + block, f32),
            pltpu.VMEM(block, f32),
            pltpu.VMEM((STEPS,) + block, f32),
            pltpu.VMEM(block, f32),
            pltpu.VMEM((total, total), bf16),
            pltpu.VMEM((total, total), bf16),
            pltpu.VMEM((width, total), bf16),
            pltpu.VMEM((width, total), bf16),
            dma((6 + STEPS,)),
            dma((24,)),
            dma((24,)),
            dma((24,)),
            dma((24,)),
            dma((8,)),
            dma((8,)),
        ]
        + bufs,
        compiler_params=pltpu.CompilerParams(
            collective_id=0, has_side_effects=True, vmem_limit_bytes=56 * MIB
        ),
        name="predict",
    )(
        centers,
        coefs.T,
        eigvecs,
        eig_weights.reshape(1, eigs),
        landmark_index.reshape(1, -1),
        batch_index,
        targets.transpose(0, 2, 1),
    )

    tile = count // STEPS
    new_coefs, residuals = pl.pallas_call(
        update_kernel,
        grid=(STEPS,),
        out_shape=[
            jax.ShapeDtypeStruct((outputs, count), f32),
            jax.ShapeDtypeStruct((STEPS, outputs, rows), f32),
        ],
        in_specs=[
            pl.BlockSpec((total, tile), lambda i: (0, i)),
            pl.BlockSpec((total, tile), lambda i: (0, i)),
            pl.BlockSpec((outputs, tile), lambda i: (0, i)),
            pl.BlockSpec((STEPS, outputs, rows), lambda i: (0, 0, 0)),
        ],
        out_specs=[
            pl.BlockSpec((outputs, tile), lambda i: (0, i)),
            pl.BlockSpec((1, outputs, rows), lambda i: (i, 0, 0)),
        ],
        scratch_shapes=[pltpu.VMEM((outputs, total), bf16)] * 2,
        compiler_params=pltpu.CompilerParams(vmem_limit_bytes=60 * MIB),
        name="update",
    )(update_high, update_low, coefs.T, residual)
    return new_coefs.T, residuals.transpose(0, 2, 1)


def solution(mesh, sizes=SIZES):
    in_specs = (
        P(("grp", "ctr"), None),
        P(("grp", "ctr"), None),
        P(("grp", "ctr"), None),
        P(),
        P(("grp", "ctr")),
        P(),
        P(),
    )
    out_specs = (P(("grp", "ctr"), None), P())
    return jax.shard_map(
        functools.partial(body, sizes),
        mesh=mesh,
        in_specs=in_specs,
        out_specs=out_specs,
        check_vma=False,
    )
```
